128 devices in a mesh: decode: 16 (over x, y), pool: 8 (over z, core).
Axes of the slice: x: 4, y: 4, z: 4, core: 2. Of those that a mesh axis runs over, the one named last changes fastest.
Arguments:
- q_nope: bfloat16 [8192, 8192], P('decode', 'pool'), may hold values from -6 to 6
- q_rope: bfloat16 [8192, 4096], P('decode', 'pool'), may hold values from -8 to 8
- up_keys: bfloat16 [64, 128, 512], P('pool'), may hold values from -0.5 to 0.5
- up_values: bfloat16 [64, 512, 128], P('pool'), may hold values from -1 to 1
- page_pool: bfloat16 [4096, 64, 576], P(('decode', 'pool')), may hold values from -6 to 6
- page_table: int32 [128, 16], P('decode'), may hold values from 0 to 4095, as said below
- lengths: int32 [128], P('decode'), may hold values from 1 to 1024, 81920 in all
- prefix_latent: bfloat16 [384, 576], P('decode'), may hold values from -8 to 8
- tree_latent: bfloat16 [8192, 576], P('decode'), may hold values from -6 to 6
- parents: int32 [128, 64], P('decode'), may hold values from 0 to 62, as said below
Outputs:
- attended: bfloat16 [8192, 8192], P('decode', 'pool')
The draws below stay inside these ranges and needn't reach their ends.
Inputs may be any that keep to these rules, and one draw needn't show every extreme that they name: `page_table`: entry (q, j) is the global number of page j of request q, which holds context positions j * 64 to (j + 1) * 64 - 1. Page n lies on device n // 32 of decode+pool (decode index slowest) as its local page n % 32. No two entries name the same page. The pages of one decode group's 8 requests lie at most 2 on any one device, and exactly 2 on some. parents[q, 0] = 0 for the root; every other node names an earlier node.
All inputs are finite; a program needn't handle non-finite values. No bound on the sum of `lengths` on one device may be relied on, other than what follows from the above.
Results may differ from the reference program's by a relative error of at most 0.0075.
Values may be sent and summed in bfloat16 or wider, within the bound.
No kernel may reach another device: no remote copies, remote signals or barrier semaphores. Data moves between devices by JAX's collectives and lax.ppermute only.
A program may use at most 128 MiB of HBM per device.

```python
import math
import jax
import jax.numpy as jnp
import numpy as np
from jax import lax

H = 64
DN = 128
DR = 64
DL = 512
DV = 128
PAGE = 64
PPR = 16
TREE = 64
PREFIX = 384
REQ = 8
LAT = 576
CTX = 1024
GROUPS = 16
OWNERS = 128
REQS = 128
ROWS = 8192
CAPACITY = 2
POOL_DEV = 32


def draw_q_rope(key, part):
    key = jax.random.fold_in(key, 31)
    return jnp.clip(jax.random.normal(key, (ROWS, H * DR), jnp.float32), -6.0, 6.0).astype(jnp.bfloat16)


def draw_prefix_latent(key, part):
    key = jax.random.fold_in(key, 37)
    return jnp.clip(jax.random.normal(key, (PREFIX, LAT), jnp.float32), -6.0, 6.0).astype(jnp.bfloat16)


def draw_parents(key, part):
    key = jax.random.fold_in(key, 23)
    nodes = jnp.arange(TREE, dtype=jnp.int32)
    upper = jnp.maximum(nodes, 1)
    picks = jax.random.randint(key, (REQS, TREE), 0, upper[None, :])
    requests = jnp.arange(REQS, dtype=jnp.int32)[:, None]
    forced = (nodes[None, :] == TREE - 1) & (requests % 4 == 0)
    picks = jnp.where(forced, TREE - 2, picks)
    return jnp.where(nodes[None, :] == 0, 0, picks).astype(jnp.int32)


def draw_page_table(key, part):
    key = jax.random.fold_in(key, 11)
    group_pages = REQ * PPR
    owner_keys = jax.random.split(jax.random.fold_in(key, 1), OWNERS)
    slot_perm = jax.vmap(lambda single: jax.random.permutation(single, POOL_DEV))(owner_keys).astype(jnp.int32)
    slot_perm = slot_perm.at[OWNERS - 1].set(POOL_DEV - 1 - jnp.arange(POOL_DEV, dtype=jnp.int32))
    owner_grid = jnp.repeat(jnp.arange(OWNERS, dtype=jnp.int32), CAPACITY)
    slot_grid = jnp.tile(jnp.arange(CAPACITY, dtype=jnp.int32), OWNERS)

    def one_group(group):
        group_key = jax.random.fold_in(key, 100 + group)
        order = jax.random.permutation(jax.random.fold_in(group_key, 1), OWNERS).astype(jnp.int32)
        position = jnp.zeros((OWNERS,), jnp.int32).at[order].set(jnp.arange(OWNERS, dtype=jnp.int32))
        last_position = position[OWNERS - 1]
        swapped = jnp.where(position == 0, last_position, position).at[OWNERS - 1].set(0)
        position = jnp.where(group == 0, swapped, position)
        counts = jnp.where(position < OWNERS // 4, CAPACITY, jnp.where(position < 3 * OWNERS // 4, CAPACITY // 2, 0))
        live = slot_grid < counts[owner_grid]
        sort_key = jnp.where(live, 0, 1) * (OWNERS * CAPACITY) + jnp.arange(OWNERS * CAPACITY, dtype=jnp.int32)
        picked = jnp.argsort(sort_key)[:group_pages]
        shuffle = jax.random.permutation(jax.random.fold_in(group_key, 2), group_pages)
        picked = picked[shuffle]
        owner = owner_grid[picked]
        within = slot_grid[picked]
        local_page = slot_perm[owner, group * CAPACITY + within]
        return (owner * POOL_DEV + local_page).reshape(REQ, PPR)
    tables = jax.vmap(one_group)(jnp.arange(GROUPS, dtype=jnp.int32))
    return tables.reshape(REQS, PPR).astype(jnp.int32)


def shard_levels(own_key, extent, cuts, smallest, top_value):
    loudness, own = 1.0, jax.random.fold_in(own_key, 6)
    for dim, parts in cuts:
        draws = jnp.exp(jax.random.uniform(jax.random.fold_in(own, dim), (parts,), jnp.float32, smallest / len(cuts), top_value / len(cuts)))
        loudness = loudness * jnp.repeat(draws, extent[dim] // parts).reshape([-1 if axis == dim else 1 for axis in range(len(extent))])
    return loudness


def profile(number_of, total, most, skew):
    portions = [(1 << 20) // math.isqrt(standing ** skew) + 1 for standing in range(2, number_of + 1)]
    spare, given = total - most - (number_of - 1), [1] * (number_of - 1)
    while spare > 0:
        movable = [i for i in range(number_of - 1) if given[i] < most]
        mass, budget = sum([portions[i] for i in movable]), spare
        for i in movable:
            more = min(most - given[i], max(1, budget * portions[i] // mass), spare)
            given[i] = given[i] + more
            spare = spare - more
    return np.array([most] + given)


def uneven(own_key, amount, total, limit, slope):
    if amount == 2:
        one = jax.random.randint(own_key, (), max(1, total - limit), min(limit, total - 1) + 1)
        return jnp.stack([one, total - one])
    sizes = jnp.asarray(profile(amount, total, limit, slope), jnp.int32)
    couples = (amount - 1) // 2
    donor, receiver = sizes[1:1 + 2 * couples:2], sizes[2:2 + 2 * couples:2]
    slack = jnp.minimum(donor - 1, limit - receiver)
    moved = jax.random.randint(jax.random.fold_in(own_key, 1), (couples,), 0, 1 << 20) % (slack + 1)
    sizes = sizes.at[1:1 + 2 * couples:2].set(donor - moved).at[2:2 + 2 * couples:2].set(receiver + moved)
    return sizes[jax.random.permutation(jax.random.fold_in(own_key, 2), amount)]


def bell_draw(key, extent, spread, most, pieces=(), kind=jnp.bfloat16):
    array = jax.random.normal(key, extent, jnp.float32) * spread
    if len(pieces) > 0:
        array = shard_levels(key, extent, pieces, -0.22, 0.18) * array
    return jnp.clip(array, min=-most, max=most).astype(kind)


def setup_inputs(seed: int = 0) -> dict:
    arg_keys = jax.random.split(jax.random.key(seed), 11)
    return {
        "q_nope": bell_draw(arg_keys[0], (ROWS, H * DN), 1.0, 6.0, ((0, 16), (1, 8))),
        "q_rope": draw_q_rope(jax.random.fold_in(arg_keys[10], 71), 0),
        "up_keys": bell_draw(arg_keys[2], (H, DN, DL), DN ** -0.5, 0.5, ((0, 8),)),
        "up_values": bell_draw(arg_keys[3], (H, DL, DV), (DL // 16) ** -0.5, 1.0, ((0, 8),)),
        "page_pool": bell_draw(arg_keys[4], (OWNERS * POOL_DEV, PAGE, LAT), 1.0, 6.0, ((0, 128),)),
        "page_table": draw_page_table(jax.random.fold_in(arg_keys[10], 71), 0),
        "lengths": uneven(arg_keys[6], REQS, REQS * CTX * 5 // 8, CTX, 2).astype(jnp.int32),
        "prefix_latent": draw_prefix_latent(jax.random.fold_in(arg_keys[10], 71), 0),
        "tree_latent": bell_draw(arg_keys[8], (ROWS, LAT), 1.0, 6.0, ((0, 16),)),
        "parents": draw_parents(jax.random.fold_in(arg_keys[10], 71), 0),
    }


def ancestry(parent_row):
    size = parent_row.shape[0]
    nodes = jnp.arange(size, dtype=jnp.int32)
    links = (parent_row[:, None] == nodes[None, :]).astype(jnp.int32)
    reach = jnp.maximum(links, (nodes[:, None] == nodes[None, :]).astype(jnp.int32))
    for sweep in range(max(1, (size - 1).bit_length())):
        reach = jnp.minimum(jnp.dot(reach, reach), 1)
    return reach > 0


def reference(q_nope, q_rope, up_keys, up_values, page_pool, page_table, lengths, prefix_latent, tree_latent, parents):
    scale = (DN + DR) ** -0.5
    keys_up = up_keys.astype(jnp.float32)
    values_up = up_values.astype(jnp.float32)
    prefix = prefix_latent.astype(jnp.float32)
    position = jnp.arange(CTX, dtype=jnp.int32)

    def one_request(index):
        start = (index * TREE).astype(jnp.int32)
        nope_rows = lax.dynamic_slice_in_dim(q_nope, start, TREE, 0).reshape(TREE, H, DN).astype(jnp.float32)
        absorbed = jnp.einsum("thn,hnl->thl", nope_rows, keys_up)
        absorbed = lax.optimization_barrier(absorbed.astype(jnp.bfloat16)).astype(jnp.float32)
        rope_rows = lax.dynamic_slice_in_dim(q_rope, start, TREE, 0).reshape(TREE, H, DR).astype(jnp.float32)
        context = page_pool[page_table[index]].reshape(CTX, LAT).astype(jnp.float32)
        tree = lax.dynamic_slice_in_dim(tree_latent, start, TREE, 0).astype(jnp.float32)

        def scores(keys):
            return (jnp.einsum("thl,kl->thk", absorbed, keys[:, :DL]) + jnp.einsum("thd,kd->thk", rope_rows, keys[:, DL:])) * scale

        prefix_scores = scores(prefix)
        context_scores = scores(context)
        tree_scores = scores(tree)
        context_seen = (position < lengths[index])[None, None, :]
        tree_seen = ancestry(parents[index])[:, None, :]
        lowest = jnp.float32(-jnp.inf)
        top = jnp.maximum(jnp.max(prefix_scores, axis=2), jnp.max(jnp.where(context_seen, context_scores, lowest), axis=2))
        top = jnp.maximum(top, jnp.max(jnp.where(tree_seen, tree_scores, lowest), axis=2))[:, :, None]
        weights_prefix = jnp.exp(prefix_scores - top).astype(jnp.bfloat16)
        weights_context = jnp.where(context_seen, jnp.exp(context_scores - top), 0.0).astype(jnp.bfloat16)
        weights_tree = jnp.where(tree_seen, jnp.exp(tree_scores - top), 0.0).astype(jnp.bfloat16)
        weights_prefix = lax.optimization_barrier(weights_prefix).astype(jnp.float32)
        weights_context = lax.optimization_barrier(weights_context).astype(jnp.float32)
        weights_tree = lax.optimization_barrier(weights_tree).astype(jnp.float32)
        total = jnp.sum(weights_prefix, axis=2) + jnp.sum(weights_context, axis=2) + jnp.sum(weights_tree, axis=2)
        mixed = jnp.einsum("thk,kl->thl", weights_prefix, prefix[:, :DL])
        mixed = mixed + jnp.einsum("thk,kl->thl", weights_context, context[:, :DL])
        mixed = mixed + jnp.einsum("thk,kl->thl", weights_tree, tree[:, :DL])
        latent_out = (mixed / total[:, :, None]).astype(jnp.bfloat16)
        latent_out = lax.optimization_barrier(latent_out).astype(jnp.float32)
        result = jnp.einsum("thl,hlv->thv", latent_out, values_up)
        return result.astype(jnp.bfloat16).reshape(TREE, H * DV)

    outputs = lax.map(one_request, jnp.arange(REQS, dtype=jnp.int32))
    return outputs.reshape(ROWS, H * DV)
```

```python
import functools
import math

import jax
import jax.numpy as jnp
from jax import lax
from jax.experimental import pallas as pl
from jax.experimental.pallas import tpu as pltpu
from jax.sharding import PartitionSpec as P

F32 = jnp.float32
BF16 = jnp.bfloat16
VMEM_LIMIT = 48 * 1024 * 1024


def nt_dot(a, b):
    return lax.dot_general(a, b, (((1,), (1,)), ((), ())), preferred_element_type=F32)


def prepare_kernel(rows_ref, rope_ref, keys_ref, parents_ref, q_ref, seen_ref):
    head = pl.program_id(0)
    latent = keys_ref.shape[2]
    absorbed = jnp.dot(rows_ref[...], keys_ref[0], preferred_element_type=F32)
    q_ref[0, :, :latent] = absorbed.astype(BF16)
    pair = rope_ref[...].astype(F32)
    lane = lax.broadcasted_iota(jnp.int32, pair.shape, 1)
    half = pair.shape[1] // 2
    turned = pltpu.roll(pair, half, 1)
    even = lax.rem(head, 2) == 0
    source = jnp.where(even, pair, turned)
    other = jnp.where(even, turned, pair)
    q_ref[0, :, latent : latent + 2 * half] = jnp.where(lane < half, source, 0.0).astype(BF16)
    q_ref[0, :, latent + 2 * half :] = jnp.where(lane >= half, other, 0.0).astype(BF16)
    size = parents_ref.shape[1]
    columns = lax.broadcasted_iota(jnp.int32, (size, size), 1)
    rows = lax.broadcasted_iota(jnp.int32, (size, size), 0)
    links = (parents_ref[0] == columns) | (rows == columns)
    reach = links.astype(F32)
    for sweep in range(max(1, (size - 1).bit_length())):
        reach = jnp.minimum(
            jnp.dot(reach.astype(BF16), reach.astype(BF16), preferred_element_type=F32), 1.0
        )
    lowest = jnp.full((size, size), -jnp.inf, F32)
    seen_ref[0] = jnp.concatenate([jnp.where(reach > 0.5, 0.0, lowest), lowest], axis=1)


def prepare(q_nope, q_rope, up_keys, parents):
    heads, nope, latent = up_keys.shape
    rows = q_nope.shape[0]
    requests, size = parents.shape
    rope = q_rope.shape[1] // heads
    return pl.pallas_call(
        prepare_kernel,
        grid=(heads,),
        in_specs=[
            pl.BlockSpec((rows, nope), lambda h: (0, h)),
            pl.BlockSpec((rows, 2 * rope), lambda h: (0, h // 2)),
            pl.BlockSpec((1, nope, latent), lambda h: (h, 0, 0)),
            pl.BlockSpec((1, size, 1), lambda h: (h, 0, 0)),
        ],
        out_specs=[
            pl.BlockSpec((1, rows, latent + 4 * rope), lambda h: (h, 0, 0)),
            pl.BlockSpec((1, size, 2 * size), lambda h: (h, 0, 0)),
        ],
        out_shape=[
            jax.ShapeDtypeStruct((heads, rows, latent + 4 * rope), BF16),
            jax.ShapeDtypeStruct((requests, size, 2 * size), F32),
        ],
        cost_estimate=pl.CostEstimate(
            flops=2 * rows * heads * nope * latent, bytes_accessed=10_000_000, transcendentals=0
        ),
        compiler_params=pltpu.CompilerParams(vmem_limit_bytes=VMEM_LIMIT),
        name="prepare",
    )(q_nope, q_rope, up_keys, parents[:, :, None])


def pack_kernel(wanted_ref, pool_ref, out_ref):
    groups = wanted_ref.shape[0]
    shares = out_ref.shape[0] // groups
    latent = 512
    rope = pool_ref.shape[2] - latent

    def body(group, carry):
        first = pool_ref.at[pl.ds(wanted_ref[group, 0] * shares, shares)]
        second = pool_ref.at[pl.ds(wanted_ref[group, 1] * shares, shares)]
        out = out_ref.at[pl.ds(group * shares, shares)]
        out[:, :, :latent] = first[:, :, :latent]
        out[:, :, latent : 2 * latent] = second[:, :, :latent]
        out[:, :, 2 * latent :] = jnp.concatenate(
            [first[:, :, latent:], second[:, :, latent:]], axis=2
        )
        return carry

    lax.fori_loop(0, groups, body, 0)


def pack(wanted, pool, shares):
    groups = wanted.shape[0]
    eighth = pool.shape[1] // shares
    width = pool.shape[2]
    return pl.pallas_call(
        pack_kernel,
        in_specs=[
            pl.BlockSpec(memory_space=pltpu.SMEM),
            pl.BlockSpec(memory_space=pltpu.VMEM),
        ],
        out_specs=pl.BlockSpec(memory_space=pltpu.VMEM),
        out_shape=jax.ShapeDtypeStruct((groups * shares, eighth, 2 * width), BF16),
        cost_estimate=pl.CostEstimate(flops=0, bytes_accessed=5_000_000, transcendentals=0),
        compiler_params=pltpu.CompilerParams(vmem_limit_bytes=VMEM_LIMIT),
        name="pack",
    )(wanted, pool.reshape(pool.shape[0] * shares, eighth, width))


def compact_kernel(source_ref, slot_ref, got_ref, after_ref, out_ref):
    pairs = out_ref.shape[0]
    per = 8
    latent = 512
    half = (out_ref.shape[2] - 2 * latent) // 2

    def body(k, carry):
        request = k // per
        first = request * (2 * per) + lax.rem(k, per)
        ropes = []
        for side, entry in enumerate((first, first + per)):
            source = source_ref[entry]
            slot = slot_ref[entry]
            start = pl.multiple_of(slot * latent, latent)
            out_ref[k, :, side * latent : (side + 1) * latent] = got_ref[
                source, :, pl.ds(start, latent)
            ]
            both = got_ref[source, :, 2 * latent :].astype(F32)
            ropes.append(jnp.where(slot == side, both, pltpu.roll(both, half, 1)))
        lane = lax.broadcasted_iota(jnp.int32, ropes[0].shape, 1)
        out_ref[k, :, 2 * latent :] = jnp.where(lane < half, ropes[0], ropes[1]).astype(BF16)
        return carry

    lax.fori_loop(0, pairs, body, 0, unroll=4)


def compact(source, slot, got, after):
    entries = source.shape[0]
    return pl.pallas_call(
        compact_kernel,
        in_specs=[
            pl.BlockSpec(memory_space=pltpu.SMEM),
            pl.BlockSpec(memory_space=pltpu.SMEM),
            pl.BlockSpec(memory_space=pltpu.VMEM),
            pl.BlockSpec(memory_space=pl.ANY),
        ],
        out_specs=pl.BlockSpec(memory_space=pltpu.VMEM),
        out_shape=jax.ShapeDtypeStruct((entries // 2,) + got.shape[1:], BF16),
        cost_estimate=pl.CostEstimate(flops=0, bytes_accessed=4_000_000, transcendentals=0),
        compiler_params=pltpu.CompilerParams(vmem_limit_bytes=VMEM_LIMIT),
        name="compact",
    )(source, slot, got, after)


def base_kernel(scale, q_ref, prefix_ref, tree_ref, seen_ref, stats_ref, sum_ref, lat_ref, rope_ref):
    heads, size, wide = q_ref.shape
    latent = prefix_ref.shape[1] - 128
    twice = (wide - latent) // 2
    shared = prefix_ref.shape[0]
    count = lat_ref.shape[0]
    factor = scale * math.log2(math.e)
    some = 4
    block = some * size

    @pl.when(pl.program_id(0) == 0)
    def _():
        lat_ref[:shared, :] = prefix_ref[:, :latent]
        rope_ref[:shared, :] = prefix_ref[:, latent:]
        lat_ref[shared + size :, :] = jnp.zeros((count - shared - size, latent), BF16)
        rope_ref[shared + size :, :] = jnp.zeros((count - shared - size, twice), BF16)

    lat_ref[shared : shared + size, :] = tree_ref[:, :latent]
    rope_ref[shared : shared + size, :] = tree_ref[:, latent:]
    hidden = jnp.concatenate([seen_ref[0]] * some, axis=0)
    lane = lax.broadcasted_iota(jnp.int32, (block, 128), 1)
    for step in range(heads // some):
        which = slice(step * some, (step + 1) * some)
        rows = slice(step * block, (step + 1) * block)
        q = q_ref[which, :, :latent].reshape(block, latent)
        q_rope = q_ref[which, :, latent : latent + twice].reshape(block, twice)
        scores = nt_dot(q, lat_ref[...]) + nt_dot(q_rope, rope_ref[...])
        scores = jnp.concatenate([scores[:, :shared], scores[:, shared:] + hidden], axis=1)
        top = jnp.max(scores, axis=1, keepdims=True)
        weights = jnp.exp2((scores - top) * factor)
        total = jnp.sum(weights, axis=1, keepdims=True)
        sum_ref[0, rows, :] = jnp.dot(
            weights.astype(BF16), lat_ref[...], preferred_element_type=F32
        )
        stats_ref[0, rows, :] = jnp.where(lane < 64, top, total)


def base(scale, q, prefix, tree, seen):
    heads, total_rows, wide = q.shape
    requests, size = seen.shape[:2]
    latent = prefix.shape[1] - 128
    rows = heads * size
    count = prefix.shape[0] + 2 * size
    return pl.pallas_call(
        functools.partial(base_kernel, scale),
        grid=(requests,),
        in_specs=[
            pl.BlockSpec((heads, size, wide), lambda i: (0, i, 0)),
            pl.BlockSpec(prefix.shape, lambda i: (0, 0)),
            pl.BlockSpec((size, tree.shape[1]), lambda i: (i, 0)),
            pl.BlockSpec((1, size, 2 * size), lambda i: (i, 0, 0)),
        ],
        out_specs=[
            pl.BlockSpec((1, rows, 128), lambda i: (i, 0, 0)),
            pl.BlockSpec((1, rows, latent), lambda i: (i, 0, 0)),
        ],
        out_shape=[
            jax.ShapeDtypeStruct((requests, rows, 128), F32),
            jax.ShapeDtypeStruct((requests, rows, latent), F32),
        ],
        scratch_shapes=[pltpu.VMEM((count, latent), BF16), pltpu.VMEM((count, 128), BF16)],
        cost_estimate=pl.CostEstimate(
            flops=2 * requests * rows * count * (2 * latent + 64),
            bytes_accessed=requests * rows * (latent * 6 + 1024),
            transcendentals=requests * rows * count,
        ),
        compiler_params=pltpu.CompilerParams(vmem_limit_bytes=VMEM_LIMIT),
        name="base",
    )(q, prefix, tree, seen)


def context_kernel(
    scale, lengths_ref, q_ref, pages_ref, stats_ref, sum_ref, values_ref, out_ref, mixed_ref
):
    heads, size, wide = q_ref.shape
    latent = values_ref.shape[1]
    twice = (wide - latent) // 2
    shares, per, _ = pages_ref.shape
    request = pl.program_id(0)
    length = lengths_ref[request]
    factor = scale * math.log2(math.e)
    lowest = F32(-jnp.inf)
    some = 4
    block = some * size
    part = per // 2
    section = shares * part

    column = lax.broadcasted_iota(jnp.int32, (1, section), 1)
    position = (column % part) // 8 * 64 + column // part * 8 + column % 8

    def keys(index, start, stop):
        half = index % 2
        return pages_ref[:, half * part : (half + 1) * part, start:stop].reshape(
            section, stop - start
        )

    def work(sections):
        for step in range(heads // some):
            which = slice(step * some, (step + 1) * some)
            rows = slice(step * block, (step + 1) * block)
            q = q_ref[which, :, :latent].reshape(block, latent)
            scores = []
            for index in range(sections):
                side = index // 2
                q_rope = q_ref[
                    which, :, latent + side * twice : latent + (side + 1) * twice
                ].reshape(block, twice)
                score = nt_dot(q, keys(index, side * latent, (side + 1) * latent))
                score = score + nt_dot(q_rope, keys(index, 2 * latent, 2 * latent + twice))
                if index == sections - 1:
                    score = jnp.where(position + index * section < length, score, lowest)
                scores.append(score)
            before = stats_ref[0, rows, :1]
            peak = functools.reduce(jnp.maximum, scores)
            top = jnp.maximum(before, jnp.max(peak, axis=1, keepdims=True))
            fade = jnp.exp2((before - top) * factor)
            total = stats_ref[0, rows, 64:65] * fade
            mixed = sum_ref[0, rows, :] * fade
            gained = None
            for index in range(sections):
                side = index // 2
                weights = jnp.exp2((scores[index] - top) * factor)
                gained = weights if gained is None else gained + weights
                mixed = mixed + jnp.dot(
                    weights.astype(BF16),
                    keys(index, side * latent, (side + 1) * latent),
                    preferred_element_type=F32,
                )
            total = total + jnp.sum(gained, axis=1, keepdims=True)
            final = (mixed / total).astype(BF16).reshape(some, size, latent)
            mixed_ref[which, pl.ds(pl.multiple_of(request * size, size), size), :] = final

    count = pl.cdiv(length, section)
    for sections in range(1, 5):

        @pl.when(count == sections)
        def _():
            work(sections)

    value = values_ref.shape[2]

    @pl.when(request == pl.num_programs(0) - 1)
    def _():
        for head in range(heads):
            out_ref[:, head * value : (head + 1) * value] = jnp.dot(
                mixed_ref[head], values_ref[head], preferred_element_type=F32
            ).astype(BF16)


def context(scale, lengths, q, pages, stats, sums, up_values):
    heads, total_rows, wide = q.shape
    requests, rows, latent = sums.shape
    size = rows // heads
    value = up_values.shape[2]
    shares, all_rows, width = pages.shape
    per = all_rows // requests
    grid_spec = pltpu.PrefetchScalarGridSpec(
        num_scalar_prefetch=1,
        grid=(requests,),
        in_specs=[
            pl.BlockSpec((heads, size, wide), lambda i, *_: (0, i, 0)),
            pl.BlockSpec((shares, per, width), lambda i, *_: (0, i, 0)),
            pl.BlockSpec((1, rows, 128), lambda i, *_: (i, 0, 0)),
            pl.BlockSpec((1, rows, latent), lambda i, *_: (i, 0, 0)),
            pl.BlockSpec(up_values.shape, lambda i, *_: (0, 0, 0)),
        ],
        out_specs=pl.BlockSpec((total_rows, heads * value), lambda i, *_: (0, 0)),
        scratch_shapes=[pltpu.VMEM((heads, total_rows, latent), BF16)],
    )
    count = 2 * shares * per
    return pl.pallas_call(
        functools.partial(context_kernel, scale),
        grid_spec=grid_spec,
        out_shape=jax.ShapeDtypeStruct((total_rows, heads * value), BF16),
        cost_estimate=pl.CostEstimate(
            flops=2 * requests * rows * count * (2 * latent + 64),
            bytes_accessed=requests * rows * latent * 8,
            transcendentals=requests * rows * count,
        ),
        compiler_params=pltpu.CompilerParams(vmem_limit_bytes=VMEM_LIMIT),
        name="context",
    )(lengths, q, pages, stats, sums, up_values)


def local(
    q_nope,
    q_rope,
    up_keys,
    up_values,
    page_pool,
    page_table,
    lengths,
    prefix_latent,
    tree_latent,
    parents,
):
    heads, nope_dim, latent_dim = up_keys.shape
    rope_dim = q_rope.shape[1] // heads
    scale = (nope_dim + rope_dim) ** (-0.5)
    groups = lax.axis_size("decode")
    shares = lax.axis_size("pool")
    pool_local = page_pool.shape[0]
    width = page_pool.shape[2]
    me = lax.axis_index("pool")

    flat = page_table.reshape(-1)
    entries = flat.shape[0]
    owner_of = flat // pool_local
    order = jnp.arange(entries, dtype=jnp.int32)
    owners = jnp.arange(groups, dtype=jnp.int32) * shares + me
    match = owner_of[None, :] == owners[:, None]
    code = order * pool_local + flat % pool_local
    first = jnp.min(jnp.where(match, code[None, :], entries * pool_local), axis=1)
    last = jnp.max(jnp.where(match, code[None, :], 0), axis=1)
    asks = jnp.stack([first, last], axis=1) % pool_local
    wanted = lax.all_to_all(asks, "decode", split_axis=0, concat_axis=0, tiled=True)
    earlier = (order[None, :] < order[:, None]) & (owner_of[None, :] == owner_of[:, None])
    slot_of = jnp.any(earlier, axis=1).astype(jnp.int32)

    wide = latent_dim + 2 * rope_dim
    prefix = prefix_latent
    step = 1
    while step < groups:
        pairs = [(i, i ^ step) for i in range(groups)]
        prefix = jnp.concatenate([prefix, lax.ppermute(prefix, "decode", pairs)], axis=0)
        step *= 2
    prefix = jnp.pad(prefix, ((0, 0), (0, wide - width)))
    tree = jnp.pad(tree_latent, ((0, 0), (0, wide - width)))

    packed = pack(wanted, page_pool, shares)
    got = lax.all_to_all(packed, ("decode", "pool"), split_axis=0, concat_axis=0, tiled=True)
    q, seen = prepare(q_nope, q_rope, up_keys, parents)
    mine = compact(owner_of, slot_of, got, seen)
    pages = lax.all_gather(mine.reshape(-1, 2 * width), "pool", axis=0, tiled=False)
    stats, sums = base(scale, q, prefix, tree, seen)
    return context(scale, lengths, q, pages, stats, sums, up_values)


def solution(mesh):
    in_specs = (
        P("decode", "pool"),
        P("decode", "pool"),
        P("pool", None, None),
        P("pool", None, None),
        P(("decode", "pool"), None, None),
        P("decode", None),
        P("decode"),
        P("decode", None),
        P("decode", None),
        P("decode", None),
    )
    out_specs = P("decode", "pool")
    return jax.shard_map(local, mesh=mesh, in_specs=in_specs, out_specs=out_specs, check_vma=False)
```

```python
import functools
import math

import jax
import jax.numpy as jnp
from jax import lax
from jax.experimental import pallas as pl
from jax.experimental.pallas import tpu as pltpu
from jax.sharding import PartitionSpec as P

F32 = jnp.float32
BF16 = jnp.bfloat16
VMEM_LIMIT = 48 * 1024 * 1024


def nt_dot(a, b):
    return lax.dot_general(a, b, (((1,), (1,)), ((), ())), preferred_element_type=F32)


def prepare_kernel(rows_ref, rope_ref, keys_ref, parents_ref, q_ref, seen_ref):
    head = pl.program_id(0)
    latent = keys_ref.shape[2]
    absorbed = jnp.dot(rows_ref[...], keys_ref[0], preferred_element_type=F32)
    q_ref[0, :, :latent] = absorbed.astype(BF16)
    pair = rope_ref[...].astype(F32)
    lane = lax.broadcasted_iota(jnp.int32, pair.shape, 1)
    half = pair.shape[1] // 2
    turned = pltpu.roll(pair, half, 1)
    even = lax.rem(head, 2) == 0
    source = jnp.where(even, pair, turned)
    other = jnp.where(even, turned, pair)
    q_ref[0, :, latent : latent + 2 * half] = jnp.where(lane < half, source, 0.0).astype(BF16)
    q_ref[0, :, latent + 2 * half :] = jnp.where(lane >= half, other, 0.0).astype(BF16)
    size = parents_ref.shape[1]
    columns = lax.broadcasted_iota(jnp.int32, (size, size), 1)
    rows = lax.broadcasted_iota(jnp.int32, (size, size), 0)
    links = (parents_ref[0] == columns) | (rows == columns)
    reach = links.astype(F32)
    for sweep in range(max(1, (size - 1).bit_length())):
        reach = jnp.minimum(
            jnp.dot(reach.astype(BF16), reach.astype(BF16), preferred_element_type=F32), 1.0
        )
    lowest = jnp.full((size, size), -jnp.inf, F32)
    seen_ref[0] = jnp.concatenate([jnp.where(reach > 0.5, 0.0, lowest), lowest], axis=1)


def prepare(q_nope, q_rope, up_keys, parents):
    heads, nope, latent = up_keys.shape
    rows = q_nope.shape[0]
    requests, size = parents.shape
    rope = q_rope.shape[1] // heads
    return pl.pallas_call(
        prepare_kernel,
        grid=(heads,),
        in_specs=[
            pl.BlockSpec((rows, nope), lambda h: (0, h)),
            pl.BlockSpec((rows, 2 * rope), lambda h: (0, h // 2)),
            pl.BlockSpec((1, nope, latent), lambda h: (h, 0, 0)),
            pl.BlockSpec((1, size, 1), lambda h: (h, 0, 0)),
        ],
        out_specs=[
            pl.BlockSpec((1, rows, latent + 4 * rope), lambda h: (h, 0, 0)),
            pl.BlockSpec((1, size, 2 * size), lambda h: (h, 0, 0)),
        ],
        out_shape=[
            jax.ShapeDtypeStruct((heads, rows, latent + 4 * rope), BF16),
            jax.ShapeDtypeStruct((requests, size, 2 * size), F32),
        ],
        cost_estimate=pl.CostEstimate(
            flops=2 * rows * heads * nope * latent, bytes_accessed=10_000_000, transcendentals=0
        ),
        compiler_params=pltpu.CompilerParams(vmem_limit_bytes=VMEM_LIMIT),
        name="prepare",
    )(q_nope, q_rope, up_keys, parents[:, :, None])


def pack_kernel(wanted_ref, pool_ref, out_ref):
    groups = wanted_ref.shape[0]
    shares = out_ref.shape[0] // groups
    latent = 512
    rope = pool_ref.shape[2] - latent

    def body(group, carry):
        first = pool_ref.at[pl.ds(wanted_ref[group, 0] * shares, shares)]
        second = pool_ref.at[pl.ds(wanted_ref[group, 1] * shares, shares)]
        out = out_ref.at[pl.ds(group * shares, shares)]
        out[:, :, :latent] = first[:, :, :latent]
        out[:, :, latent : 2 * latent] = second[:, :, :latent]
        out[:, :, 2 * latent :] = jnp.concatenate(
            [first[:, :, latent:], second[:, :, latent:]], axis=2
        )
        return carry

    lax.fori_loop(0, groups, body, 0)


def pack(wanted, pool, shares):
    groups = wanted.shape[0]
    eighth = pool.shape[1] // shares
    width = pool.shape[2]
    return pl.pallas_call(
        pack_kernel,
        in_specs=[
            pl.BlockSpec(memory_space=pltpu.SMEM),
            pl.BlockSpec(memory_space=pltpu.VMEM),
        ],
        out_specs=pl.BlockSpec(memory_space=pltpu.VMEM),
        out_shape=jax.ShapeDtypeStruct((groups * shares, eighth, 2 * width), BF16),
        cost_estimate=pl.CostEstimate(flops=0, bytes_accessed=5_000_000, transcendentals=0),
        compiler_params=pltpu.CompilerParams(vmem_limit_bytes=VMEM_LIMIT),
        name="pack",
    )(wanted, pool.reshape(pool.shape[0] * shares, eighth, width))


def compact_kernel(source_ref, slot_ref, got_ref, after_ref, out_ref):
    pairs = out_ref.shape[0]
    per = 8
    latent = 512
    half = (out_ref.shape[2] - 2 * latent) // 2

    def body(k, carry):
        request = k // per
        first = request * (2 * per) + lax.rem(k, per)
        ropes = []
        for side, entry in enumerate((first, first + per)):
            source = source_ref[entry]
            slot = slot_ref[entry]
            start = pl.multiple_of(slot * latent, latent)
            out_ref[k, :, side * latent : (side + 1) * latent] = got_ref[
                source, :, pl.ds(start, latent)
            ]
            both = got_ref[source, :, 2 * latent :].astype(F32)
            ropes.append(jnp.where(slot == side, both, pltpu.roll(both, half, 1)))
        lane = lax.broadcasted_iota(jnp.int32, ropes[0].shape, 1)
        out_ref[k, :, 2 * latent :] = jnp.where(lane < half, ropes[0], ropes[1]).astype(BF16)
        return carry

    lax.fori_loop(0, pairs, body, 0, unroll=4)


def compact(source, slot, got, after):
    entries = source.shape[0]
    return pl.pallas_call(
        compact_kernel,
        in_specs=[
            pl.BlockSpec(memory_space=pltpu.SMEM),
            pl.BlockSpec(memory_space=pltpu.SMEM),
            pl.BlockSpec(memory_space=pltpu.VMEM),
            pl.BlockSpec(memory_space=pltpu.SMEM),
        ],
        out_specs=pl.BlockSpec(memory_space=pltpu.VMEM),
        out_shape=jax.ShapeDtypeStruct((entries // 2,) + got.shape[1:], BF16),
        cost_estimate=pl.CostEstimate(flops=0, bytes_accessed=4_000_000, transcendentals=0),
        compiler_params=pltpu.CompilerParams(vmem_limit_bytes=VMEM_LIMIT),
        name="compact",
    )(source, slot, got, after)


def spread(column, width):
    if width <= 128:
        return column[:, :width]
    return jnp.concatenate([column] * (width // 128), axis=1)


def attend_kernel(scale, picks, shared, halves, finish, lengths_ref, shares_ref, q_ref, *refs):
    refs = list(refs)
    taken = [refs.pop(0) for _ in range(3)]
    pieces = [
        (refs.pop(0), refs.pop(0)) if halves else (refs.pop(0),) for _ in range(len(picks))
    ]
    values_ref = refs.pop(0) if finish else None
    if finish:
        out_ref, keys_ref, mixed_ref = refs
    else:
        top_out, total_out, sum_out, keys_ref = refs
    heads, size, wide = q_ref.shape
    latent = wide - 256
    part = pieces[0][0].shape[0] // 2
    section = len(picks) * part
    origin = keys_ref.shape[0] - 4 * section
    request = pl.program_id(0)
    length = lengths_ref[request]
    factor = scale * math.log2(math.e)
    lowest = F32(-jnp.inf)
    some = 8
    block = some * size

    @pl.when(request == 0)
    def _():
        keys_ref[:, latent:] = jnp.zeros((keys_ref.shape[0], 256), BF16)
        if shared:
            prompt = taken[0].shape[0]
            keys_ref[:prompt, : latent + 128] = taken[0][...]
            keys_ref[prompt + size : origin, :latent] = jnp.zeros(
                (origin - prompt - size, latent), BF16
            )

    if shared:
        prompt = taken[0].shape[0]
        keys_ref[prompt : prompt + size, : latent + 128] = taken[1][...]
    for which, refs_of in enumerate(pieces):
        piece = refs_of[0][...]
        if halves:
            piece = jnp.where(request < pl.num_programs(0) // 2, piece, refs_of[1][...])
        for index in range(4):
            side, half = index // 2, index % 2
            rows = slice(
                origin + index * section + which * part,
                origin + index * section + (which + 1) * part,
            )
            some_rows = piece[half * part : (half + 1) * part]
            keys_ref[rows, :latent] = some_rows[:, side * latent : (side + 1) * latent]
            keys_ref[rows, latent + side * 128 : latent + (side + 1) * 128] = some_rows[
                :, 2 * latent :
            ]

    def work(sections):
        count = sections * section
        column = lax.broadcasted_iota(jnp.int32, (1, count), 1)
        position = column // section * 256 + column % part // 8 * 64 + column % 8
        for which, pick in enumerate(picks):
            position = position + jnp.where(
                column // part % len(picks) == which, shares_ref[pick] * 8, 0
            )
        bias = jnp.where(position < length, 0.0, lowest)
        if shared:
            hidden = jnp.concatenate([taken[2][0]] * some, axis=0)
        for step in range(heads // some):
            which = slice(step * some, (step + 1) * some)
            rows = slice(step * block, (step + 1) * block)
            q = q_ref[which].reshape(block, wide)
            scores = nt_dot(q, keys_ref[origin : origin + count, :]) + bias
            if shared:
                first = nt_dot(q, keys_ref[:prompt, :])
                tree = nt_dot(q, keys_ref[prompt:origin, :]) + hidden
                scores = jnp.concatenate([first, tree, scores], axis=1)
            top = jnp.broadcast_to(jnp.max(scores, axis=1, keepdims=True), (block, 128))
            if not shared:
                before = taken[0][0, rows, :]
                top = jnp.maximum(top, before)
                fade = jnp.exp2((before - top) * factor)
            weights = jnp.exp2((scores - spread(top, scores.shape[1])) * factor)
            total = jnp.broadcast_to(jnp.sum(weights, axis=1, keepdims=True), (block, 128))
            mixed = jnp.dot(
                weights.astype(BF16),
                keys_ref[0 if shared else origin : origin + count, :latent],
                preferred_element_type=F32,
            )
            if not shared:
                total = total + taken[1][0, rows, :] * fade
                mixed = mixed + taken[2][0, rows, :] * spread(fade, latent)
            if finish:
                mixed = mixed * spread(1.0 / total, latent)
                mixed_ref[which, pl.ds(pl.multiple_of(request * size, size), size), :] = (
                    mixed.astype(BF16).reshape(some, size, latent)
                )
            else:
                top_out[0, rows, :] = top
                total_out[0, rows, :] = total
                sum_out[0, rows, :] = mixed

    needed = pl.cdiv(length, 256)
    steps = (1, 2, 3, 4) if section % 128 == 0 else (2, 4)
    for low, high in zip((0,) + steps, steps):

        @pl.when((needed > low) & (needed <= high))
        def _():
            work(high)

    if finish:
        value = values_ref.shape[2]

        @pl.when(request == pl.num_programs(0) - 1)
        def _():
            for head in range(heads):
                out_ref[:, head * value : (head + 1) * value] = jnp.dot(
                    mixed_ref[head], values_ref[head], preferred_element_type=F32
                ).astype(BF16)


def attend(name, scale, lengths, shares, picks, q, shared, given, pieces, up_values=None):
    heads, total_rows, wide = q.shape
    requests = lengths.shape[0]
    size = total_rows // requests
    rows = heads * size
    latent = wide - 256
    halves = isinstance(pieces[0], tuple)
    finish = up_values is not None
    flat = [array for piece in pieces for array in (piece if halves else (piece,))]
    per = flat[0].shape[0] * (2 if halves else 1) // requests
    width = flat[0].shape[1]
    half = requests // 2
    origin = given[0].shape[0] + 2 * size if shared else 0
    count = origin + 2 * per * len(pieces)

    state_specs = [
        pl.BlockSpec((1, rows, 128), lambda i, *_: (i, 0, 0)),
        pl.BlockSpec((1, rows, 128), lambda i, *_: (i, 0, 0)),
        pl.BlockSpec((1, rows, latent), lambda i, *_: (i, 0, 0)),
    ]
    in_specs = [pl.BlockSpec((heads, size, wide), lambda i, *_: (0, i, 0))]
    if shared:
        in_specs += [
            pl.BlockSpec(given[0].shape, lambda i, *_: (0, 0)),
            pl.BlockSpec((size, given[1].shape[1]), lambda i, *_: (i, 0)),
            pl.BlockSpec((1, size, 2 * size), lambda i, *_: (i, 0, 0)),
        ]
    else:
        in_specs += state_specs
    for _ in pieces:
        if halves:
            in_specs.append(
                pl.BlockSpec((per, width), lambda i, *_: (jnp.minimum(i, half - 1), 0))
            )
            in_specs.append(pl.BlockSpec((per, width), lambda i, *_: (jnp.maximum(i - half, 0), 0)))
        else:
            in_specs.append(pl.BlockSpec((per, width), lambda i, *_: (i, 0)))
    operands = [lengths, shares, q, *given, *flat]
    scratch = [pltpu.VMEM((count, wide), BF16)]
    if finish:
        value = up_values.shape[2]
        operands.append(up_values)
        in_specs.append(pl.BlockSpec(up_values.shape, lambda i, *_: (0, 0, 0)))
        out_specs = pl.BlockSpec((total_rows, heads * value), lambda i, *_: (0, 0))
        out_shape = jax.ShapeDtypeStruct((total_rows, heads * value), BF16)
        scratch.append(pltpu.VMEM((heads, total_rows, latent), BF16))
    else:
        out_specs = state_specs
        out_shape = [
            jax.ShapeDtypeStruct((requests, rows, 128), F32),
            jax.ShapeDtypeStruct((requests, rows, 128), F32),
            jax.ShapeDtypeStruct((requests, rows, latent), F32),
        ]
    return pl.pallas_call(
        functools.partial(attend_kernel, scale, picks, shared, halves, finish),
        grid_spec=pltpu.PrefetchScalarGridSpec(
            num_scalar_prefetch=2,
            grid=(requests,),
            in_specs=in_specs,
            out_specs=out_specs,
            scratch_shapes=scratch,
        ),
        out_shape=out_shape,
        cost_estimate=pl.CostEstimate(
            flops=2 * requests * rows * count * (2 * latent + 64),
            bytes_accessed=requests * rows * latent * 8,
            transcendentals=requests * rows * count,
        ),
        compiler_params=pltpu.CompilerParams(vmem_limit_bytes=VMEM_LIMIT),
        name=name,
    )(*operands)


def local(
    q_nope,
    q_rope,
    up_keys,
    up_values,
    page_pool,
    page_table,
    lengths,
    prefix_latent,
    tree_latent,
    parents,
):
    heads, nope_dim, latent_dim = up_keys.shape
    rope_dim = q_rope.shape[1] // heads
    scale = (nope_dim + rope_dim) ** (-0.5)
    groups = lax.axis_size("decode")
    shares = lax.axis_size("pool")
    pool_local = page_pool.shape[0]
    width = page_pool.shape[2]
    me = lax.axis_index("pool")

    flat = page_table.reshape(-1)
    entries = flat.shape[0]
    owner_of = flat // pool_local
    order = jnp.arange(entries, dtype=jnp.int32)
    owners = jnp.arange(groups, dtype=jnp.int32) * shares + me
    match = owner_of[None, :] == owners[:, None]
    code = order * pool_local + flat % pool_local
    first = jnp.min(jnp.where(match, code[None, :], entries * pool_local), axis=1)
    last = jnp.max(jnp.where(match, code[None, :], 0), axis=1)
    asks = jnp.stack([first, last], axis=1) % pool_local
    wanted = lax.all_to_all(asks, "decode", split_axis=0, concat_axis=0, tiled=True)
    earlier = (order[None, :] < order[:, None]) & (owner_of[None, :] == owner_of[:, None])
    slot_of = jnp.any(earlier, axis=1).astype(jnp.int32)

    wide = latent_dim + 2 * rope_dim
    prefix = prefix_latent
    step = 1
    while step < groups:
        pairs = [(i, i ^ step) for i in range(groups)]
        prefix = jnp.concatenate([prefix, lax.ppermute(prefix, "decode", pairs)], axis=0)
        step *= 2
    prefix = jnp.pad(prefix, ((0, 0), (0, wide - width)))
    tree = jnp.pad(tree_latent, ((0, 0), (0, wide - width)))

    packed = pack(wanted, page_pool, shares)
    got = lax.all_to_all(packed, ("decode", "pool"), split_axis=0, concat_axis=0, tiled=True)
    q, hidden = prepare(q_nope, q_rope, up_keys, parents)
    after = hidden[0, :1, :1] + prefix[-1:, :1].astype(F32)
    own = compact(owner_of, slot_of, got, after).reshape(-1, 2 * width)

    swap = [(i, i ^ 1) for i in range(shares)]
    up = [(i, (i + 2) % shares) for i in range(shares)]
    down = [(i, (i - 2) % shares) for i in range(shares)]
    me = lax.axis_index("pool")
    other = me + 1 - 2 * (me % 2)
    at = [me, other, me - 2, me + 2, other - 2, other + 2, me + 4, other + 4]
    at = jnp.stack([place % shares for place in at]).astype(jnp.int32)
    below = lax.ppermute(own, "pool", up)
    above = lax.ppermute(own, "pool", down)
    beside = lax.ppermute(own, "pool", swap)
    state = attend(
        "first", scale, lengths, at, (0, 1), q, True, (prefix, tree, hidden), [own, beside]
    )
    below, above, state = lax.optimization_barrier((below, above, state))
    middle = own.shape[0] // 2
    far_up = lax.ppermute(below[:middle], "pool", up)
    far_down = lax.ppermute(above[middle:], "pool", down)
    below_beside = lax.ppermute(below, "pool", swap)
    above_beside = lax.ppermute(above, "pool", swap)
    state = attend(
        "second",
        scale,
        lengths,
        at,
        (2, 3, 4, 5),
        q,
        False,
        state,
        [below, above, below_beside, above_beside],
    )
    far_up, far_down, state = lax.optimization_barrier((far_up, far_down, state))
    far_up_beside = lax.ppermute(far_up, "pool", swap)
    far_down_beside = lax.ppermute(far_down, "pool", swap)
    return attend(
        "third",
        scale,
        lengths,
        at,
        (6, 7),
        q,
        False,
        state,
        [(far_up, far_down), (far_up_beside, far_down_beside)],
        up_values,
    )


def solution(mesh):
    in_specs = (
        P("decode", "pool"),
        P("decode", "pool"),
        P("pool", None, None),
        P("pool", None, None),
        P(("decode", "pool"), None, None),
        P("decode", None),
        P("decode"),
        P("decode", None),
        P("decode", None),
        P("decode", None),
    )
    out_specs = P("decode", "pool")
    return jax.shard_map(local, mesh=mesh, in_specs=in_specs, out_specs=out_specs, check_vma=False)
```

```python
import functools
import math

import jax
import jax.numpy as jnp
from jax import lax
from jax.experimental import pallas as pl
from jax.experimental.pallas import tpu as pltpu
from jax.sharding import PartitionSpec as P

F32 = jnp.float32
BF16 = jnp.bfloat16
VMEM_LIMIT = 24 * 1024 * 1024


def nt_dot(a, b):
    return lax.dot_general(a, b, (((1,), (1,)), ((), ())), preferred_element_type=F32)


def prepare_kernel(rows_ref, rope_ref, keys_ref, parents_ref, q_ref, seen_ref):
    head = pl.program_id(0)
    latent = keys_ref.shape[2]
    absorbed = jnp.dot(rows_ref[...], keys_ref[0], preferred_element_type=F32)
    q_ref[0, :, :latent] = absorbed.astype(BF16)
    pair = rope_ref[...].astype(F32)
    lane = lax.broadcasted_iota(jnp.int32, pair.shape, 1)
    half = pair.shape[1] // 2
    turned = pltpu.roll(pair, half, 1)
    even = lax.rem(head, 2) == 0
    source = jnp.where(even, pair, turned)
    other = jnp.where(even, turned, pair)
    q_ref[0, :, latent : latent + 2 * half] = jnp.where(lane < half, source, 0.0).astype(BF16)
    q_ref[0, :, latent + 2 * half :] = jnp.where(lane >= half, other, 0.0).astype(BF16)
    size = parents_ref.shape[1]
    columns = lax.broadcasted_iota(jnp.int32, (size, size), 1)
    rows = lax.broadcasted_iota(jnp.int32, (size, size), 0)
    links = (parents_ref[0] == columns) | (rows == columns)
    reach = links.astype(F32)
    for sweep in range(max(1, (size - 1).bit_length())):
        reach = jnp.minimum(
            jnp.dot(reach.astype(BF16), reach.astype(BF16), preferred_element_type=F32), 1.0
        )
    lowest = jnp.full((size, size), -jnp.inf, F32)
    seen_ref[0] = jnp.concatenate([jnp.where(reach > 0.5, 0.0, lowest), lowest], axis=1)


def prepare(q_nope, q_rope, up_keys, parents):
    heads, nope, latent = up_keys.shape
    rows = q_nope.shape[0]
    requests, size = parents.shape
    rope = q_rope.shape[1] // heads
    return pl.pallas_call(
        prepare_kernel,
        grid=(heads,),
        in_specs=[
            pl.BlockSpec((rows, nope), lambda h: (0, h)),
            pl.BlockSpec((rows, 2 * rope), lambda h: (0, h // 2)),
            pl.BlockSpec((1, nope, latent), lambda h: (h, 0, 0)),
            pl.BlockSpec((1, size, 1), lambda h: (h, 0, 0)),
        ],
        out_specs=[
            pl.BlockSpec((1, rows, latent + 4 * rope), lambda h: (h, 0, 0)),
            pl.BlockSpec((1, size, 2 * size), lambda h: (h, 0, 0)),
        ],
        out_shape=[
            jax.ShapeDtypeStruct((heads, rows, latent + 4 * rope), BF16),
            jax.ShapeDtypeStruct((requests, size, 2 * size), F32),
        ],
        cost_estimate=pl.CostEstimate(
            flops=2 * rows * heads * nope * latent, bytes_accessed=10_000_000, transcendentals=0
        ),
        compiler_params=pltpu.CompilerParams(vmem_limit_bytes=VMEM_LIMIT),
        name="prepare",
    )(q_nope, q_rope, up_keys, parents[:, :, None])


def pack_kernel(wanted_ref, pool_ref, out_ref):
    groups = wanted_ref.shape[0]
    shares = out_ref.shape[0] // groups
    latent = 512
    rope = pool_ref.shape[2] - latent

    def body(group, carry):
        first = pool_ref.at[pl.ds(wanted_ref[group, 0] * shares, shares)]
        second = pool_ref.at[pl.ds(wanted_ref[group, 1] * shares, shares)]
        out = out_ref.at[pl.ds(group * shares, shares)]
        out[:, :, :latent] = first[:, :, :latent]
        out[:, :, latent : 2 * latent] = second[:, :, :latent]
        out[:, :, 2 * latent :] = jnp.concatenate(
            [first[:, :, latent:], second[:, :, latent:]], axis=2
        )
        return carry

    lax.fori_loop(0, groups, body, 0)


def pack(wanted, pool, shares):
    groups = wanted.shape[0]
    eighth = pool.shape[1] // shares
    width = pool.shape[2]
    return pl.pallas_call(
        pack_kernel,
        in_specs=[
            pl.BlockSpec(memory_space=pltpu.SMEM),
            pl.BlockSpec(memory_space=pltpu.VMEM),
        ],
        out_specs=pl.BlockSpec(memory_space=pltpu.VMEM),
        out_shape=jax.ShapeDtypeStruct((groups * shares, eighth, 2 * width), BF16),
        cost_estimate=pl.CostEstimate(flops=0, bytes_accessed=5_000_000, transcendentals=0),
        compiler_params=pltpu.CompilerParams(vmem_limit_bytes=VMEM_LIMIT),
        name="pack",
    )(wanted, pool.reshape(pool.shape[0] * shares, eighth, width))


def compact_kernel(source_ref, slot_ref, got_ref, after_ref, out_ref):
    pairs = out_ref.shape[0]
    per = 8
    latent = 512
    half = (out_ref.shape[2] - 2 * latent) // 2

    def body(k, carry):
        request = k // per
        first = request * (2 * per) + lax.rem(k, per)
        ropes = []
        for side, entry in enumerate((first, first + per)):
            source = source_ref[entry]
            slot = slot_ref[entry]
            start = pl.multiple_of(slot * latent, latent)
            out_ref[k, :, side * latent : (side + 1) * latent] = got_ref[
                source, :, pl.ds(start, latent)
            ]
            both = got_ref[source, :, 2 * latent :].astype(F32)
            ropes.append(jnp.where(slot == side, both, pltpu.roll(both, half, 1)))
        lane = lax.broadcasted_iota(jnp.int32, ropes[0].shape, 1)
        out_ref[k, :, 2 * latent :] = jnp.where(lane < half, ropes[0], ropes[1]).astype(BF16)
        return carry

    lax.fori_loop(0, pairs, body, 0, unroll=4)


def compact(source, slot, got, after):
    entries = source.shape[0]
    return pl.pallas_call(
        compact_kernel,
        in_specs=[
            pl.BlockSpec(memory_space=pltpu.SMEM),
            pl.BlockSpec(memory_space=pltpu.SMEM),
            pl.BlockSpec(memory_space=pltpu.VMEM),
            pl.BlockSpec(memory_space=pltpu.SMEM),
        ],
        out_specs=pl.BlockSpec(memory_space=pltpu.VMEM),
        out_shape=jax.ShapeDtypeStruct((entries // 2,) + got.shape[1:], BF16),
        cost_estimate=pl.CostEstimate(flops=0, bytes_accessed=4_000_000, transcendentals=0),
        compiler_params=pltpu.CompilerParams(vmem_limit_bytes=VMEM_LIMIT),
        name="compact",
    )(source, slot, got, after)


def spread(column, width):
    if width <= 128:
        return column[:, :width]
    return jnp.concatenate([column] * (width // 128), axis=1)


def attend_kernel(scale, picks, shared, halves, finish, lengths_ref, shares_ref, q_ref, *refs):
    refs = list(refs)
    taken = [refs.pop(0) for _ in range(3)]
    pieces = [
        (refs.pop(0), refs.pop(0)) if halves else (refs.pop(0),) for _ in range(len(picks))
    ]
    values_ref = refs.pop(0) if finish else None
    if finish:
        out_ref, keys_ref, mixed_ref = refs
    else:
        top_out, total_out, sum_out, keys_ref = refs
    heads, total_rows, wide = q_ref.shape
    size = total_rows // lengths_ref.shape[0]
    latent = wide - 256
    part = pieces[0][0].shape[0] // 2
    section = len(picks) * part
    origin = keys_ref.shape[0] - 4 * section
    request = pl.program_id(0)
    length = lengths_ref[request]
    factor = scale * math.log2(math.e)
    lowest = F32(-jnp.inf)
    some = 8
    block = some * size

    @pl.when(request == 0)
    def _():
        keys_ref[:, latent:] = jnp.zeros((keys_ref.shape[0], 256), BF16)
        if shared:
            prompt = taken[0].shape[0]
            keys_ref[:prompt, : latent + 128] = taken[0][...]
            keys_ref[prompt + size : origin, :latent] = jnp.zeros(
                (origin - prompt - size, latent), BF16
            )

    if shared:
        prompt = taken[0].shape[0]
        keys_ref[prompt : prompt + size, : latent + 128] = taken[1][...]
    for which, refs_of in enumerate(pieces):
        piece = refs_of[0][...]
        if halves:
            piece = jnp.where(request < pl.num_programs(0) // 2, piece, refs_of[1][...])
        for index in range(4):
            side, half = index // 2, index % 2
            rows = slice(
                origin + index * section + which * part,
                origin + index * section + (which + 1) * part,
            )
            some_rows = piece[half * part : (half + 1) * part]
            keys_ref[rows, :latent] = some_rows[:, side * latent : (side + 1) * latent]
            keys_ref[rows, latent + side * 128 : latent + (side + 1) * 128] = some_rows[
                :, 2 * latent :
            ]

    def work(sections):
        count = sections * section
        column = lax.broadcasted_iota(jnp.int32, (1, count), 1)
        position = column // section * 256 + column % part // 8 * 64 + column % 8
        for which, pick in enumerate(picks):
            position = position + jnp.where(
                column // part % len(picks) == which, shares_ref[pick] * 8, 0
            )
        bias = jnp.where(position < length, 0.0, lowest)
        if shared:
            hidden = jnp.concatenate([taken[2][0]] * some, axis=0)
        for step in range(heads // some):
            which = slice(step * some, (step + 1) * some)
            rows = slice(step * block, (step + 1) * block)
            q = q_ref[which, pl.ds(pl.multiple_of(request * size, size), size), :]
            q = q.reshape(block, wide)
            scores = nt_dot(q, keys_ref[origin : origin + count, :]) + bias
            if shared:
                first = nt_dot(q, keys_ref[:prompt, :])
                tree = nt_dot(q, keys_ref[prompt:origin, :]) + hidden
                scores = jnp.concatenate([first, tree, scores], axis=1)
            top = jnp.broadcast_to(jnp.max(scores, axis=1, keepdims=True), (block, 128))
            if not shared:
                before = taken[0][request, rows, :]
                top = jnp.maximum(top, before)
                fade = jnp.exp2((before - top) * factor)
            weights = jnp.exp2((scores - spread(top, scores.shape[1])) * factor)
            total = jnp.broadcast_to(jnp.sum(weights, axis=1, keepdims=True), (block, 128))
            mixed = jnp.dot(
                weights.astype(BF16),
                keys_ref[0 if shared else origin : origin + count, :latent],
                preferred_element_type=F32,
            )
            if not shared:
                total = total + taken[1][request, rows, :] * fade
                mixed = mixed + taken[2][request, rows, :].astype(F32) * spread(fade, latent)
            if finish:
                mixed = mixed * spread(1.0 / total, latent)
                mixed_ref[which, pl.ds(pl.multiple_of(request * size, size), size), :] = (
                    mixed.astype(BF16).reshape(some, size, latent)
                )
            else:
                top_out[request, rows, :] = top
                total_out[request, rows, :] = total
                sum_out[request, rows, :] = mixed.astype(BF16)

    needed = pl.cdiv(length, 256)
    steps = (1, 2, 3, 4) if section % 128 == 0 else (2, 4)
    for low, high in zip((0,) + steps, steps):

        @pl.when((needed > low) & (needed <= high))
        def _():
            work(high)

    if finish:
        value = values_ref.shape[2]

        @pl.when(request == pl.num_programs(0) - 1)
        def _():
            for head in range(heads):
                out_ref[:, head * value : (head + 1) * value] = jnp.dot(
                    mixed_ref[head], values_ref[head], preferred_element_type=F32
                ).astype(BF16)


def attend(name, scale, lengths, shares, picks, q, shared, given, pieces, up_values=None):
    heads, total_rows, wide = q.shape
    requests = lengths.shape[0]
    size = total_rows // requests
    rows = heads * size
    latent = wide - 256
    halves = isinstance(pieces[0], tuple)
    finish = up_values is not None
    flat = [array for piece in pieces for array in (piece if halves else (piece,))]
    per = flat[0].shape[0] * (2 if halves else 1) // requests
    width = flat[0].shape[1]
    half = requests // 2
    origin = given[0].shape[0] + 2 * size if shared else 0
    count = origin + 2 * per * len(pieces)

    whole = pl.BlockSpec(memory_space=pltpu.VMEM)
    state_specs = [whole, whole, whole]
    in_specs = [whole]
    if shared:
        in_specs += [
            pl.BlockSpec(given[0].shape, lambda i, *_: (0, 0)),
            pl.BlockSpec((size, given[1].shape[1]), lambda i, *_: (i, 0)),
            pl.BlockSpec((1, size, 2 * size), lambda i, *_: (i, 0, 0)),
        ]
    else:
        in_specs += state_specs
    for _ in pieces:
        if halves:
            in_specs.append(
                pl.BlockSpec((per, width), lambda i, *_: (jnp.minimum(i, half - 1), 0))
            )
            in_specs.append(pl.BlockSpec((per, width), lambda i, *_: (jnp.maximum(i - half, 0), 0)))
        else:
            in_specs.append(pl.BlockSpec((per, width), lambda i, *_: (i, 0)))
    operands = [lengths, shares, q, *given, *flat]
    scratch = [pltpu.VMEM((count, wide), BF16)]
    if finish:
        value = up_values.shape[2]
        operands.append(up_values)
        in_specs.append(whole)
        out_specs = pl.BlockSpec((total_rows, heads * value), lambda i, *_: (0, 0))
        out_shape = jax.ShapeDtypeStruct((total_rows, heads * value), BF16)
        scratch.append(pltpu.VMEM((heads, total_rows, latent), BF16))
    else:
        out_specs = state_specs
        out_shape = [
            jax.ShapeDtypeStruct((requests, rows, 128), F32),
            jax.ShapeDtypeStruct((requests, rows, 128), F32),
            jax.ShapeDtypeStruct((requests, rows, latent), BF16),
        ]
    return pl.pallas_call(
        functools.partial(attend_kernel, scale, picks, shared, halves, finish),
        grid_spec=pltpu.PrefetchScalarGridSpec(
            num_scalar_prefetch=2,
            grid=(requests,),
            in_specs=in_specs,
            out_specs=out_specs,
            scratch_shapes=scratch,
        ),
        out_shape=out_shape,
        input_output_aliases={} if shared or finish else {3: 0, 4: 1, 5: 2},
        cost_estimate=pl.CostEstimate(
            flops=2 * requests * rows * count * (2 * latent + 64),
            bytes_accessed=requests * rows * latent * 8,
            transcendentals=requests * rows * count,
        ),
        compiler_params=pltpu.CompilerParams(vmem_limit_bytes=VMEM_LIMIT),
        name=name,
    )(*operands)


def local(
    q_nope,
    q_rope,
    up_keys,
    up_values,
    page_pool,
    page_table,
    lengths,
    prefix_latent,
    tree_latent,
    parents,
):
    heads, nope_dim, latent_dim = up_keys.shape
    rope_dim = q_rope.shape[1] // heads
    scale = (nope_dim + rope_dim) ** (-0.5)
    groups = lax.axis_size("decode")
    shares = lax.axis_size("pool")
    pool_local = page_pool.shape[0]
    width = page_pool.shape[2]
    me = lax.axis_index("pool")

    flat = page_table.reshape(-1)
    entries = flat.shape[0]
    owner_of = flat // pool_local
    order = jnp.arange(entries, dtype=jnp.int32)
    owners = jnp.arange(groups, dtype=jnp.int32) * shares + me
    match = owner_of[None, :] == owners[:, None]
    code = order * pool_local + flat % pool_local
    first = jnp.min(jnp.where(match, code[None, :], entries * pool_local), axis=1)
    last = jnp.max(jnp.where(match, code[None, :], 0), axis=1)
    asks = jnp.stack([first, last], axis=1) % pool_local
    prompt = prefix_latent.reshape(-1, 128)
    held = prompt.shape[0]
    message = jnp.concatenate(
        [
            jnp.broadcast_to(prompt[None], (groups,) + prompt.shape),
            jnp.pad(asks.astype(BF16)[:, None, :], ((0, 0), (0, 3), (0, 126))),
        ],
        axis=1,
    )
    message = lax.all_to_all(message, "decode", split_axis=0, concat_axis=0, tiled=True)
    wanted = message[:, held, :2].astype(jnp.int32)
    prefix = message[:, :held].reshape(-1, width)
    earlier = (order[None, :] < order[:, None]) & (owner_of[None, :] == owner_of[:, None])
    slot_of = jnp.any(earlier, axis=1).astype(jnp.int32)

    wide = latent_dim + 2 * rope_dim
    tree = jnp.pad(tree_latent, ((0, 0), (0, wide - width)))

    packed = pack(wanted, page_pool, shares)
    got = lax.all_to_all(packed, ("decode", "pool"), split_axis=0, concat_axis=0, tiled=True)
    q, hidden = prepare(q_nope, q_rope, up_keys, parents)
    prefix = jnp.pad(prefix, ((0, 0), (0, wide - width)))
    after = hidden[0, :1, :1] + (prefix[:1, :1] + tree[:1, :1]).astype(F32)
    own = compact(owner_of, slot_of, got, after).reshape(-1, 2 * width)

    swap = [(i, i ^ 1) for i in range(shares)]
    up = [(i, (i + 2) % shares) for i in range(shares)]
    down = [(i, (i - 2) % shares) for i in range(shares)]
    me = lax.axis_index("pool")
    other = me + 1 - 2 * (me % 2)
    at = [me, other, me - 2, me + 2, other - 2, other + 2, me + 4, other + 4]
    at = jnp.stack([place % shares for place in at]).astype(jnp.int32)
    below = lax.ppermute(own, "pool", up)
    above = lax.ppermute(own, "pool", down)
    beside = lax.ppermute(own, "pool", swap)
    state = attend(
        "first", scale, lengths, at, (0, 1), q, True, (prefix, tree, hidden), [own, beside]
    )
    below, above, state = lax.optimization_barrier((below, above, state))
    middle = own.shape[0] // 2
    far_up = lax.ppermute(below[:middle], "pool", up)
    far_down = lax.ppermute(above[middle:], "pool", down)
    below_beside = lax.ppermute(below, "pool", swap)
    above_beside = lax.ppermute(above, "pool", swap)
    state = attend(
        "second",
        scale,
        lengths,
        at,
        (2, 3, 4, 5),
        q,
        False,
        state,
        [below, above, below_beside, above_beside],
    )
    far_up, far_down, state = lax.optimization_barrier((far_up, far_down, state))
    far_up_beside = lax.ppermute(far_up, "pool", swap)
    far_down_beside = lax.ppermute(far_down, "pool", swap)
    return attend(
        "third",
        scale,
        lengths,
        at,
        (6, 7),
        q,
        False,
        state,
        [(far_up, far_down), (far_up_beside, far_down_beside)],
        up_values,
    )


def solution(mesh):
    in_specs = (
        P("decode", "pool"),
        P("decode", "pool"),
        P("pool", None, None),
        P("pool", None, None),
        P(("decode", "pool"), None, None),
        P("decode", None),
        P("decode"),
        P("decode", None),
        P("decode", None),
        P("decode", None),
    )
    out_specs = P("decode", "pool")
    return jax.shard_map(local, mesh=mesh, in_specs=in_specs, out_specs=out_specs, check_vma=False)
```

```python
import functools
import math

import jax
import jax.numpy as jnp
from jax import lax
from jax.experimental import pallas as pl
from jax.experimental.pallas import tpu as pltpu
from jax.sharding import PartitionSpec as P

F32 = jnp.float32
BF16 = jnp.bfloat16
VMEM_LIMIT = 24 * 1024 * 1024


def nt_dot(a, b):
    return lax.dot_general(a, b, (((1,), (1,)), ((), ())), preferred_element_type=F32)


def prepare_kernel(rows_ref, rope_ref, keys_ref, parents_ref, q_ref, seen_ref):
    head = pl.program_id(0)
    latent = keys_ref.shape[2]
    absorbed = jnp.dot(rows_ref[...], keys_ref[0], preferred_element_type=F32)
    q_ref[0, :, :latent] = absorbed.astype(BF16)
    pair = rope_ref[...].astype(F32)
    lane = lax.broadcasted_iota(jnp.int32, pair.shape, 1)
    half = pair.shape[1] // 2
    turned = pltpu.roll(pair, half, 1)
    even = lax.rem(head, 2) == 0
    source = jnp.where(even, pair, turned)
    other = jnp.where(even, turned, pair)
    q_ref[0, :, latent : latent + 2 * half] = jnp.where(lane < half, source, 0.0).astype(BF16)
    q_ref[0, :, latent + 2 * half :] = jnp.where(lane >= half, other, 0.0).astype(BF16)
    size = parents_ref.shape[1]
    columns = lax.broadcasted_iota(jnp.int32, (size, size), 1)
    rows = lax.broadcasted_iota(jnp.int32, (size, size), 0)
    links = (parents_ref[0] == columns) | (rows == columns)
    reach = links.astype(F32)
    for sweep in range(max(1, (size - 1).bit_length())):
        reach = jnp.minimum(
            jnp.dot(reach.astype(BF16), reach.astype(BF16), preferred_element_type=F32), 1.0
        )
    lowest = jnp.full((size, size), -jnp.inf, F32)
    seen_ref[0] = jnp.concatenate([jnp.where(reach > 0.5, 0.0, lowest), lowest], axis=1)


def prepare(q_nope, q_rope, up_keys, parents):
    heads, nope, latent = up_keys.shape
    rows = q_nope.shape[0]
    requests, size = parents.shape
    rope = q_rope.shape[1] // heads
    return pl.pallas_call(
        prepare_kernel,
        grid=(heads,),
        in_specs=[
            pl.BlockSpec((rows, nope), lambda h: (0, h)),
            pl.BlockSpec((rows, 2 * rope), lambda h: (0, h // 2)),
            pl.BlockSpec((1, nope, latent), lambda h: (h, 0, 0)),
            pl.BlockSpec((1, size, 1), lambda h: (h, 0, 0)),
        ],
        out_specs=[
            pl.BlockSpec((1, rows, latent + 4 * rope), lambda h: (h, 0, 0)),
            pl.BlockSpec((1, size, 2 * size), lambda h: (h, 0, 0)),
        ],
        out_shape=[
            jax.ShapeDtypeStruct((heads, rows, latent + 4 * rope), BF16),
            jax.ShapeDtypeStruct((requests, size, 2 * size), F32),
        ],
        cost_estimate=pl.CostEstimate(
            flops=2 * rows * heads * nope * latent, bytes_accessed=10_000_000, transcendentals=0
        ),
        compiler_params=pltpu.CompilerParams(vmem_limit_bytes=VMEM_LIMIT),
        name="prepare",
    )(q_nope, q_rope, up_keys, parents[:, :, None])


def pack_kernel(wanted_ref, pool_ref, out_ref):
    size = pool_ref.shape[1]
    some = out_ref.shape[0] // size
    latent = 512
    for index in range(some):
        group = pl.program_id(0) * some + index
        first = pool_ref.at[wanted_ref[group, 0]]
        second = pool_ref.at[wanted_ref[group, 1]]
        rows = slice(index * size, (index + 1) * size)
        out_ref[rows, :latent] = first[:, :latent]
        out_ref[rows, latent : 2 * latent] = second[:, :latent]
        out_ref[rows, 2 * latent :] = jnp.concatenate(
            [first[:, latent:], second[:, latent:]], axis=1
        )


def pack(wanted, pool, shares):
    groups = wanted.shape[0]
    size, width = pool.shape[1:]
    steps = 4
    packed = pl.pallas_call(
        pack_kernel,
        grid=(steps,),
        in_specs=[
            pl.BlockSpec(memory_space=pltpu.SMEM),
            pl.BlockSpec(memory_space=pltpu.VMEM),
        ],
        out_specs=pl.BlockSpec((groups // steps * size, 2 * width), lambda i: (i, 0)),
        out_shape=pltpu.HBM((groups * size, 2 * width), BF16),
        cost_estimate=pl.CostEstimate(flops=0, bytes_accessed=5_000_000, transcendentals=0),
        compiler_params=pltpu.CompilerParams(vmem_limit_bytes=VMEM_LIMIT),
        name="pack",
    )(wanted, pool)
    return packed.reshape(groups * shares, size // shares, 2 * width)


def compact_kernel(source_ref, slot_ref, got_ref, after_ref, out_ref):
    pairs = out_ref.shape[0]
    per = 8
    latent = 512
    half = (out_ref.shape[2] - 2 * latent) // 2

    def body(k, carry):
        request = k // per
        first = request * (2 * per) + lax.rem(k, per)
        ropes = []
        for side, entry in enumerate((first, first + per)):
            source = source_ref[entry]
            slot = slot_ref[entry]
            start = pl.multiple_of(slot * latent, latent)
            out_ref[k, :, side * latent : (side + 1) * latent] = got_ref[
                source, :, pl.ds(start, latent)
            ]
            both = got_ref[source, :, 2 * latent :].astype(F32)
            ropes.append(jnp.where(slot == side, both, pltpu.roll(both, half, 1)))
        lane = lax.broadcasted_iota(jnp.int32, ropes[0].shape, 1)
        out_ref[k, :, 2 * latent :] = jnp.where(lane < half, ropes[0], ropes[1]).astype(BF16)
        return carry

    lax.fori_loop(0, pairs, body, 0, unroll=4)


def compact(source, slot, got, after):
    entries = source.shape[0]
    return pl.pallas_call(
        compact_kernel,
        in_specs=[
            pl.BlockSpec(memory_space=pltpu.SMEM),
            pl.BlockSpec(memory_space=pltpu.SMEM),
            pl.BlockSpec(memory_space=pltpu.VMEM),
            pl.BlockSpec(memory_space=pltpu.SMEM),
        ],
        out_specs=pl.BlockSpec(memory_space=pltpu.VMEM),
        out_shape=jax.ShapeDtypeStruct((entries // 2,) + got.shape[1:], BF16),
        cost_estimate=pl.CostEstimate(flops=0, bytes_accessed=4_000_000, transcendentals=0),
        compiler_params=pltpu.CompilerParams(vmem_limit_bytes=VMEM_LIMIT),
        name="compact",
    )(source, slot, got, after)


def spread(column, width):
    if width <= 128:
        return column[:, :width]
    return jnp.concatenate([column] * (width // 128), axis=1)


def attend_kernel(scale, picks, shared, halves, finish, lengths_ref, shares_ref, q_ref, *refs):
    refs = list(refs)
    taken = [refs.pop(0) for _ in range(3)]
    pieces = [
        (refs.pop(0), refs.pop(0)) if halves else (refs.pop(0),) for _ in range(len(picks))
    ]
    values_ref = refs.pop(0) if finish else None
    if finish:
        out_ref, keys_ref, mixed_ref = refs
    else:
        top_out, total_out, sum_out, keys_ref = refs
    heads, total_rows, wide = q_ref.shape
    size = total_rows // lengths_ref.shape[0]
    latent = wide - 256
    part = pieces[0][0].shape[0] // 2 // keys_ref.shape[0]
    section = len(picks) * part
    origin = keys_ref.shape[1] - 4 * section
    step_requests = keys_ref.shape[0]
    factor = scale * math.log2(math.e)
    lowest = F32(-jnp.inf)
    some = 8
    block = some * size

    @pl.when(pl.program_id(0) == 0)
    def _():
        for turn in range(step_requests):
            keys_ref[turn, :, latent:] = jnp.zeros((keys_ref.shape[1], 256), BF16)
            if shared:
                prompt = taken[0].shape[0]
                keys_ref[turn, :prompt, : latent + 128] = taken[0][...]
                keys_ref[turn, prompt + size : origin, :latent] = jnp.zeros(
                    (origin - prompt - size, latent), BF16
                )

    for turn in range(step_requests):
        if shared:
            prompt = taken[0].shape[0]
            keys_ref[turn, prompt : prompt + size, : latent + 128] = taken[1][turn * size : (turn + 1) * size]
        for which, refs_of in enumerate(pieces):
            piece = refs_of[0][turn * 2 * part : (turn + 1) * 2 * part]
            if halves:
                piece = jnp.where(pl.program_id(0) < pl.num_programs(0) // 2, piece, refs_of[1][turn * 2 * part : (turn + 1) * 2 * part])
            for index in range(4):
                side, half = index // 2, index % 2
                rows = slice(
                    origin + index * section + which * part,
                    origin + index * section + (which + 1) * part,
                )
                some_rows = piece[half * part : (half + 1) * part]
                keys_ref[turn, rows, :latent] = some_rows[:, side * latent : (side + 1) * latent]
                keys_ref[turn, rows, latent + side * 128 : latent + (side + 1) * 128] = some_rows[
                    :, 2 * latent :
                ]

    def work(turn, request, length, sections):
        count = sections * section
        column = lax.broadcasted_iota(jnp.int32, (1, count), 1)
        position = column // section * 256 + column % part // 8 * 64 + column % 8
        for which, pick in enumerate(picks):
            position = position + jnp.where(
                column // part % len(picks) == which, shares_ref[pick] * 8, 0
            )
        bias = jnp.where(position < length, 0.0, lowest)
        if shared:
            hidden = jnp.concatenate([taken[2][turn]] * some, axis=0)
        for step in range(heads // some):
            which = slice(step * some, (step + 1) * some)
            rows = slice(step * block, (step + 1) * block)
            q = q_ref[which, pl.ds(pl.multiple_of(request * size, size), size), :]
            q = q.reshape(block, wide)
            scores = nt_dot(q, keys_ref[turn, origin : origin + count, :]) + bias
            if shared:
                first = nt_dot(q, keys_ref[turn, :prompt, :])
                tree = nt_dot(q, keys_ref[turn, prompt:origin, :]) + hidden
                scores = jnp.concatenate([first, tree, scores], axis=1)
            top = jnp.broadcast_to(jnp.max(scores, axis=1, keepdims=True), (block, 128))
            if not shared:
                before = taken[0][request, rows, :]
                top = jnp.maximum(top, before)
                fade = jnp.exp2((before - top) * factor)
            weights = jnp.exp2((scores - spread(top, scores.shape[1])) * factor)
            total = jnp.broadcast_to(jnp.sum(weights, axis=1, keepdims=True), (block, 128))
            mixed = jnp.dot(
                weights.astype(BF16),
                keys_ref[turn, 0 if shared else origin : origin + count, :latent],
                preferred_element_type=F32,
            )
            if not shared:
                total = total + taken[1][request, rows, :] * fade
                mixed = mixed + taken[2][request, rows, :].astype(F32) * spread(fade, latent)
            if finish:
                mixed = mixed * spread(1.0 / total, latent)
                mixed_ref[which, pl.ds(pl.multiple_of(request * size, size), size), :] = (
                    mixed.astype(BF16).reshape(some, size, latent)
                )
            else:
                top_out[request, rows, :] = top
                total_out[request, rows, :] = total
                sum_out[request, rows, :] = mixed.astype(BF16)

    steps = (4,) if step_requests > 1 else (1, 2, 3, 4) if section % 128 == 0 else (2, 4)
    for turn in range(step_requests):
        request = pl.program_id(0) * step_requests + turn
        length = lengths_ref[request]
        needed = pl.cdiv(length, 256)
        if len(steps) == 1:
            work(turn, request, length, steps[0])
        else:
            for low, high in zip((0,) + steps, steps):

                @pl.when((needed > low) & (needed <= high))
                def _():
                    work(turn, request, length, high)

    if finish:
        value = values_ref.shape[2]

        @pl.when(pl.program_id(0) == pl.num_programs(0) - 1)
        def _():
            for head in range(heads):
                out_ref[:, head * value : (head + 1) * value] = jnp.dot(
                    mixed_ref[head], values_ref[head], preferred_element_type=F32
                ).astype(BF16)


def attend(name, scale, lengths, shares, picks, q, shared, given, pieces, up_values=None, at_once=1):
    heads, total_rows, wide = q.shape
    requests = lengths.shape[0]
    size = total_rows // requests
    rows = heads * size
    latent = wide - 256
    halves = isinstance(pieces[0], tuple)
    finish = up_values is not None
    flat = [array for piece in pieces for array in (piece if halves else (piece,))]
    per = flat[0].shape[0] * (2 if halves else 1) // requests
    width = flat[0].shape[1]
    half = requests // 2 // at_once
    origin = given[0].shape[0] + 2 * size if shared else 0
    count = origin + 2 * per * len(pieces)

    whole = pl.BlockSpec(memory_space=pltpu.VMEM)
    state_specs = [whole, whole, whole]
    in_specs = [whole]
    if shared:
        in_specs += [
            pl.BlockSpec(given[0].shape, lambda i, *_: (0, 0)),
            pl.BlockSpec((at_once * size, given[1].shape[1]), lambda i, *_: (i, 0)),
            pl.BlockSpec((at_once, size, 2 * size), lambda i, *_: (i, 0, 0)),
        ]
    else:
        in_specs += state_specs
    for _ in pieces:
        if halves:
            in_specs.append(
                pl.BlockSpec((at_once * per, width), lambda i, *_: (jnp.minimum(i, half - 1), 0))
            )
            in_specs.append(pl.BlockSpec((at_once * per, width), lambda i, *_: (jnp.maximum(i - half, 0), 0)))
        else:
            in_specs.append(pl.BlockSpec((at_once * per, width), lambda i, *_: (i, 0)))
    operands = [lengths, shares, q, *given, *flat]
    scratch = [pltpu.VMEM((at_once, count, wide), BF16)]
    if finish:
        value = up_values.shape[2]
        operands.append(up_values)
        in_specs.append(whole)
        out_specs = pl.BlockSpec((total_rows, heads * value), lambda i, *_: (0, 0))
        out_shape = jax.ShapeDtypeStruct((total_rows, heads * value), BF16)
        scratch.append(pltpu.VMEM((heads, total_rows, latent), BF16))
    else:
        out_specs = state_specs
        out_shape = [
            jax.ShapeDtypeStruct((requests, rows, 128), F32),
            jax.ShapeDtypeStruct((requests, rows, 128), F32),
            jax.ShapeDtypeStruct((requests, rows, latent), BF16),
        ]
    return pl.pallas_call(
        functools.partial(attend_kernel, scale, picks, shared, halves, finish),
        grid_spec=pltpu.PrefetchScalarGridSpec(
            num_scalar_prefetch=2,
            grid=(requests // at_once,),
            in_specs=in_specs,
            out_specs=out_specs,
            scratch_shapes=scratch,
        ),
        out_shape=out_shape,
        input_output_aliases={} if shared or finish else {3: 0, 4: 1, 5: 2},
        cost_estimate=pl.CostEstimate(
            flops=2 * requests * rows * count * (2 * latent + 64),
            bytes_accessed=requests * rows * latent * 8,
            transcendentals=requests * rows * count,
        ),
        compiler_params=pltpu.CompilerParams(vmem_limit_bytes=VMEM_LIMIT),
        name=name,
    )(*operands)


def local(
    q_nope,
    q_rope,
    up_keys,
    up_values,
    page_pool,
    page_table,
    lengths,
    prefix_latent,
    tree_latent,
    parents,
):
    heads, nope_dim, latent_dim = up_keys.shape
    rope_dim = q_rope.shape[1] // heads
    scale = (nope_dim + rope_dim) ** (-0.5)
    groups = lax.axis_size("decode")
    shares = lax.axis_size("pool")
    pool_local = page_pool.shape[0]
    width = page_pool.shape[2]
    me = lax.axis_index("pool")

    flat = page_table.reshape(-1)
    entries = flat.shape[0]
    owner_of = flat // pool_local
    order = jnp.arange(entries, dtype=jnp.int32)
    owners = jnp.arange(groups, dtype=jnp.int32) * shares + me
    match = owner_of[None, :] == owners[:, None]
    code = order * pool_local + flat % pool_local
    first = jnp.min(jnp.where(match, code[None, :], entries * pool_local), axis=1)
    last = jnp.max(jnp.where(match, code[None, :], 0), axis=1)
    asks = jnp.stack([first, last], axis=1) % pool_local
    prompt = prefix_latent.reshape(-1, 128)
    held = prompt.shape[0]
    message = jnp.concatenate(
        [
            jnp.broadcast_to(prompt[None], (groups,) + prompt.shape),
            jnp.pad(asks.astype(BF16)[:, None, :], ((0, 0), (0, 3), (0, 126))),
        ],
        axis=1,
    )
    message = lax.all_to_all(message, "decode", split_axis=0, concat_axis=0, tiled=True)
    wanted = message[:, held, :2].astype(jnp.int32)
    prefix = message[:, :held].reshape(-1, width)
    earlier = (order[None, :] < order[:, None]) & (owner_of[None, :] == owner_of[:, None])
    slot_of = jnp.any(earlier, axis=1).astype(jnp.int32)

    wide = latent_dim + 2 * rope_dim
    tree = jnp.pad(tree_latent, ((0, 0), (0, wide - width)))

    packed = pack(wanted, page_pool, shares)
    got = lax.all_to_all(packed, ("decode", "pool"), split_axis=0, concat_axis=0, tiled=True)
    q, hidden = prepare(q_nope, q_rope, up_keys, parents)
    prefix = jnp.pad(prefix, ((0, 0), (0, wide - width)))
    prefix, tree = lax.optimization_barrier((prefix, tree))
    after = hidden[0, :1, :1] + (prefix[:1, :1] + tree[:1, :1]).astype(F32)
    own = compact(owner_of, slot_of, got, after).reshape(-1, 2 * width)

    swap = [(i, i ^ 1) for i in range(shares)]
    up = [(i, (i + 2) % shares) for i in range(shares)]
    down = [(i, (i - 2) % shares) for i in range(shares)]
    me = lax.axis_index("pool")
    other = me + 1 - 2 * (me % 2)
    at = [me, other, me - 2, me + 2, other - 2, other + 2, me + 4, other + 4]
    at = jnp.stack([place % shares for place in at]).astype(jnp.int32)
    def turn(array, pairs):
        return lax.ppermute(array, "pool", pairs)

    def call(name, picks, given, pieces, **more):
        return attend(
            name, scale, lengths, at, picks, q, name == "first", given, pieces, **more
        )

    below = turn(own, up)
    above = turn(own, down)
    state = call("first", (0, 1), (prefix, tree, hidden), [own, turn(own, swap)], at_once=2)
    below, above, state = lax.optimization_barrier((below, above, state))
    middle = own.shape[0] // 2
    far_low = turn(below[:middle], up)
    far_high = turn(above[middle:], down)
    state = call(
        "second",
        (2, 3, 4, 5),
        state,
        [below, above, turn(below, swap), turn(above, swap)],
        at_once=2,
    )
    far_low, far_high, state = lax.optimization_barrier((far_low, far_high, state))
    return call(
        "third",
        (6, 7),
        state,
        [(far_low, far_high), (turn(far_low, swap), turn(far_high, swap))],
        up_values=up_values,
        at_once=4,
    )


def solution(mesh):
    in_specs = (
        P("decode", "pool"),
        P("decode", "pool"),
        P("pool", None, None),
        P("pool", None, None),
        P(("decode", "pool"), None, None),
        P("decode", None),
        P("decode"),
        P("decode", None),
        P("decode", None),
        P("decode", None),
    )
    out_specs = P("decode", "pool")
    return jax.shard_map(local, mesh=mesh, in_specs=in_specs, out_specs=out_specs, check_vma=False)
```

```python
import functools
import math

import jax
import jax.numpy as jnp
from jax import lax
from jax.experimental import pallas as pl
from jax.experimental.pallas import tpu as pltpu
from jax.sharding import PartitionSpec as P

F32 = jnp.float32
BF16 = jnp.bfloat16
VMEM_LIMIT = 24 * 1024 * 1024


def nt_dot(a, b):
    return lax.dot_general(a, b, (((1,), (1,)), ((), ())), preferred_element_type=F32)


def prepare_kernel(rows_ref, rope_ref, keys_ref, parents_ref, q_ref, seen_ref):
    head = pl.program_id(0)
    latent = keys_ref.shape[2]
    absorbed = jnp.dot(rows_ref[...], keys_ref[0], preferred_element_type=F32)
    q_ref[0, :, :latent] = absorbed.astype(BF16)
    pair = rope_ref[...].astype(F32)
    lane = lax.broadcasted_iota(jnp.int32, pair.shape, 1)
    half = pair.shape[1] // 2
    turned = pltpu.roll(pair, half, 1)
    even = lax.rem(head, 2) == 0
    source = jnp.where(even, pair, turned)
    other = jnp.where(even, turned, pair)
    q_ref[0, :, latent : latent + 2 * half] = jnp.where(lane < half, source, 0.0).astype(BF16)
    q_ref[0, :, latent + 2 * half :] = jnp.where(lane >= half, other, 0.0).astype(BF16)
    size = parents_ref.shape[1]
    columns = lax.broadcasted_iota(jnp.int32, (size, size), 1)
    rows = lax.broadcasted_iota(jnp.int32, (size, size), 0)
    links = (parents_ref[0] == columns) | (rows == columns)
    reach = links.astype(F32)
    for sweep in range(max(1, (size - 1).bit_length())):
        reach = jnp.minimum(
            jnp.dot(reach.astype(BF16), reach.astype(BF16), preferred_element_type=F32), 1.0
        )
    lowest = jnp.full((size, size), -jnp.inf, F32)
    seen_ref[0] = jnp.concatenate([jnp.where(reach > 0.5, 0.0, lowest), lowest], axis=1)


def prepare(q_nope, q_rope, up_keys, parents):
    heads, nope, latent = up_keys.shape
    rows = q_nope.shape[0]
    requests, size = parents.shape
    rope = q_rope.shape[1] // heads
    return pl.pallas_call(
        prepare_kernel,
        grid=(heads,),
        in_specs=[
            pl.BlockSpec((rows, nope), lambda h: (0, h)),
            pl.BlockSpec((rows, 2 * rope), lambda h: (0, h // 2)),
            pl.BlockSpec((1, nope, latent), lambda h: (h, 0, 0)),
            pl.BlockSpec((1, size, 1), lambda h: (h, 0, 0)),
        ],
        out_specs=[
            pl.BlockSpec((1, rows, latent + 4 * rope), lambda h: (h, 0, 0)),
            pl.BlockSpec((1, size, 2 * size), lambda h: (h, 0, 0)),
        ],
        out_shape=[
            jax.ShapeDtypeStruct((heads, rows, latent + 4 * rope), BF16),
            jax.ShapeDtypeStruct((requests, size, 2 * size), F32),
        ],
        cost_estimate=pl.CostEstimate(
            flops=2 * rows * heads * nope * latent, bytes_accessed=10_000_000, transcendentals=0
        ),
        compiler_params=pltpu.CompilerParams(vmem_limit_bytes=VMEM_LIMIT),
        name="prepare",
    )(q_nope, q_rope, up_keys, parents[:, :, None])


def compose_kernel(prompt_ref, asks_ref, pool_ref, out_ref, held_ref):
    held = prompt_ref.shape[0]
    rows = lax.broadcasted_iota(jnp.int32, (out_ref.shape[1] - held, 128), 0)
    for group in range(out_ref.shape[0]):
        out_ref[group, :held, :] = prompt_ref[...]
        asks = jnp.pad(asks_ref[group : group + 1, :].astype(F32), ((0, 0), (0, 126)))
        out_ref[group, held:, :] = jnp.where(rows == 0, asks, 0.0).astype(BF16)


def compose(prompt, asks, pool):
    rows = prompt.shape[0]
    return pl.pallas_call(
        compose_kernel,
        in_specs=[pl.BlockSpec(memory_space=pltpu.VMEM)] * 3,
        out_specs=[pl.BlockSpec(memory_space=pltpu.VMEM)] * 2,
        out_shape=[
            jax.ShapeDtypeStruct((asks.shape[0], rows + 16 - rows % 16, 128), BF16),
            jax.ShapeDtypeStruct(pool.shape, pool.dtype),
        ],
        input_output_aliases={2: 1},
        cost_estimate=pl.CostEstimate(flops=0, bytes_accessed=1_000_000, transcendentals=0),
        compiler_params=pltpu.CompilerParams(vmem_limit_bytes=VMEM_LIMIT),
        name="compose",
    )(prompt, asks, pool)


def pack_kernel(wanted_ref, pool_ref, out_ref):
    size = pool_ref.shape[1]
    some = out_ref.shape[0] // size
    latent = 512
    for index in range(some):
        group = pl.program_id(0) * some + index
        first = pool_ref.at[wanted_ref[group, 0]]
        second = pool_ref.at[wanted_ref[group, 1]]
        rows = slice(index * size, (index + 1) * size)
        out_ref[rows, :latent] = first[:, :latent]
        out_ref[rows, latent : 2 * latent] = second[:, :latent]
        out_ref[rows, 2 * latent :] = jnp.concatenate(
            [first[:, latent:], second[:, latent:]], axis=1
        )


def pack(wanted, pool, shares):
    groups = wanted.shape[0]
    size, width = pool.shape[1:]
    steps = 4
    packed = pl.pallas_call(
        pack_kernel,
        grid=(steps,),
        in_specs=[
            pl.BlockSpec(memory_space=pltpu.SMEM),
            pl.BlockSpec(memory_space=pltpu.VMEM),
        ],
        out_specs=pl.BlockSpec((groups // steps * size, 2 * width), lambda i: (i, 0)),
        out_shape=pltpu.HBM((groups * size, 2 * width), BF16),
        cost_estimate=pl.CostEstimate(flops=0, bytes_accessed=5_000_000, transcendentals=0),
        compiler_params=pltpu.CompilerParams(vmem_limit_bytes=VMEM_LIMIT),
        name="pack",
    )(wanted, pool)
    return packed.reshape(groups * shares, size // shares, 2 * width)


def compact_kernel(source_ref, slot_ref, got_ref, after_ref, out_ref):
    pairs = out_ref.shape[0]
    per = 8
    latent = 512
    half = (out_ref.shape[2] - 2 * latent) // 2

    def body(k, carry):
        request = k // per
        first = request * (2 * per) + lax.rem(k, per)
        ropes = []
        for side, entry in enumerate((first, first + per)):
            source = source_ref[entry]
            slot = slot_ref[entry]
            start = pl.multiple_of(slot * latent, latent)
            out_ref[k, :, side * latent : (side + 1) * latent] = got_ref[
                source, :, pl.ds(start, latent)
            ]
            both = got_ref[source, :, 2 * latent :].astype(F32)
            ropes.append(jnp.where(slot == side, both, pltpu.roll(both, half, 1)))
        lane = lax.broadcasted_iota(jnp.int32, ropes[0].shape, 1)
        out_ref[k, :, 2 * latent :] = jnp.where(lane < half, ropes[0], ropes[1]).astype(BF16)
        return carry

    lax.fori_loop(0, pairs, body, 0, unroll=4)


def compact(source, slot, got, after):
    entries = source.shape[0]
    return pl.pallas_call(
        compact_kernel,
        in_specs=[
            pl.BlockSpec(memory_space=pltpu.SMEM),
            pl.BlockSpec(memory_space=pltpu.SMEM),
            pl.BlockSpec(memory_space=pltpu.VMEM),
            pl.BlockSpec(memory_space=pltpu.SMEM),
        ],
        out_specs=pl.BlockSpec(memory_space=pltpu.VMEM),
        out_shape=jax.ShapeDtypeStruct((entries // 2,) + got.shape[1:], BF16),
        cost_estimate=pl.CostEstimate(flops=0, bytes_accessed=4_000_000, transcendentals=0),
        compiler_params=pltpu.CompilerParams(vmem_limit_bytes=VMEM_LIMIT),
        name="compact",
    )(source, slot, got, after)


def spread(column, width):
    if width <= 128:
        return column[:, :width]
    return jnp.concatenate([column] * (width // 128), axis=1)


def attend_kernel(scale, picks, shared, halves, finish, lengths_ref, shares_ref, q_ref, *refs):
    refs = list(refs)
    taken = [refs.pop(0) for _ in range(3)]
    pieces = [
        (refs.pop(0), refs.pop(0)) if halves else (refs.pop(0),) for _ in range(len(picks))
    ]
    values_ref = refs.pop(0) if finish else None
    if finish:
        out_ref, keys_ref, mixed_ref = refs
    else:
        top_out, total_out, sum_out, keys_ref = refs
    heads, total_rows, wide = q_ref.shape
    size = total_rows // lengths_ref.shape[0]
    latent = wide - 256
    part = pieces[0][0].shape[0] // 2 // keys_ref.shape[0]
    section = len(picks) * part
    origin = keys_ref.shape[1] - 4 * section
    step_requests = keys_ref.shape[0]
    factor = scale * math.log2(math.e)
    lowest = F32(-jnp.inf)
    some = 8
    block = some * size

    @pl.when(pl.program_id(0) == 0)
    def _():
        for turn in range(step_requests):
            keys_ref[turn, :, latent:] = jnp.zeros((keys_ref.shape[1], 256), BF16)
            if shared:
                prompt = taken[0].shape[0]
                keys_ref[turn, :prompt, : latent + 128] = taken[0][...]
                keys_ref[turn, prompt + size : origin, :latent] = jnp.zeros(
                    (origin - prompt - size, latent), BF16
                )

    for turn in range(step_requests):
        if shared:
            prompt = taken[0].shape[0]
            keys_ref[turn, prompt : prompt + size, : latent + 128] = taken[1][turn * size : (turn + 1) * size]
        for which, refs_of in enumerate(pieces):
            piece = refs_of[0][turn * 2 * part : (turn + 1) * 2 * part]
            if halves:
                piece = jnp.where(pl.program_id(0) < pl.num_programs(0) // 2, piece, refs_of[1][turn * 2 * part : (turn + 1) * 2 * part])
            for index in range(4):
                side, half = index // 2, index % 2
                rows = slice(
                    origin + index * section + which * part,
                    origin + index * section + (which + 1) * part,
                )
                some_rows = piece[half * part : (half + 1) * part]
                keys_ref[turn, rows, :latent] = some_rows[:, side * latent : (side + 1) * latent]
                keys_ref[turn, rows, latent + side * 128 : latent + (side + 1) * 128] = some_rows[
                    :, 2 * latent :
                ]

    def work(turn, request, length, sections):
        count = sections * section
        column = lax.broadcasted_iota(jnp.int32, (1, count), 1)
        position = column // section * 256 + column % part // 8 * 64 + column % 8
        for which, pick in enumerate(picks):
            position = position + jnp.where(
                column // part % len(picks) == which, shares_ref[pick] * 8, 0
            )
        bias = jnp.where(position < length, 0.0, lowest)
        if shared:
            hidden = jnp.concatenate([taken[2][turn]] * some, axis=0)
        for step in range(heads // some):
            which = slice(step * some, (step + 1) * some)
            rows = slice(step * block, (step + 1) * block)
            q = q_ref[which, pl.ds(pl.multiple_of(request * size, size), size), :]
            q = q.reshape(block, wide)
            scores = nt_dot(q, keys_ref[turn, origin : origin + count, :]) + bias
            if shared:
                first = nt_dot(q, keys_ref[turn, :prompt, :])
                tree = nt_dot(q, keys_ref[turn, prompt:origin, :]) + hidden
                scores = jnp.concatenate([first, tree, scores], axis=1)
            top = jnp.broadcast_to(jnp.max(scores, axis=1, keepdims=True), (block, 128))
            if not shared:
                before = taken[0][request, rows, :]
                top = jnp.maximum(top, before)
                fade = jnp.exp2((before - top) * factor)
            weights = jnp.exp2((scores - spread(top, scores.shape[1])) * factor)
            total = jnp.broadcast_to(jnp.sum(weights, axis=1, keepdims=True), (block, 128))
            mixed = jnp.dot(
                weights.astype(BF16),
                keys_ref[turn, 0 if shared else origin : origin + count, :latent],
                preferred_element_type=F32,
            )
            if not shared:
                total = total + taken[1][request, rows, :] * fade
                mixed = mixed + taken[2][request, rows, :].astype(F32) * spread(fade, latent)
            if finish:
                mixed = mixed * spread(1.0 / total, latent)
                mixed_ref[which, pl.ds(pl.multiple_of(request * size, size), size), :] = (
                    mixed.astype(BF16).reshape(some, size, latent)
                )
            else:
                top_out[request, rows, :] = top
                total_out[request, rows, :] = total
                sum_out[request, rows, :] = mixed.astype(BF16)

    steps = (4,) if step_requests > 1 else (1, 2, 3, 4) if section % 128 == 0 else (2, 4)
    for turn in range(step_requests):
        request = pl.program_id(0) * step_requests + turn
        length = lengths_ref[request]
        needed = pl.cdiv(length, 256)
        if len(steps) == 1:
            work(turn, request, length, steps[0])
        else:
            for low, high in zip((0,) + steps, steps):

                @pl.when((needed > low) & (needed <= high))
                def _():
                    work(turn, request, length, high)

    if finish:
        value = values_ref.shape[2]

        @pl.when(pl.program_id(0) == pl.num_programs(0) - 1)
        def _():
            for head in range(heads):
                out_ref[:, head * value : (head + 1) * value] = jnp.dot(
                    mixed_ref[head], values_ref[head], preferred_element_type=F32
                ).astype(BF16)


def attend(name, scale, lengths, shares, picks, q, shared, given, pieces, up_values=None, at_once=1):
    heads, total_rows, wide = q.shape
    requests = lengths.shape[0]
    size = total_rows // requests
    rows = heads * size
    latent = wide - 256
    halves = isinstance(pieces[0], tuple)
    finish = up_values is not None
    flat = [array for piece in pieces for array in (piece if halves else (piece,))]
    per = flat[0].shape[0] * (2 if halves else 1) // requests
    width = flat[0].shape[1]
    half = requests // 2 // at_once
    origin = given[0].shape[0] + 2 * size if shared else 0
    count = origin + 2 * per * len(pieces)

    whole = pl.BlockSpec(memory_space=pltpu.VMEM)
    state_specs = [whole, whole, whole]
    in_specs = [whole]
    if shared:
        in_specs += [
            pl.BlockSpec(given[0].shape, lambda i, *_: (0, 0)),
            pl.BlockSpec((at_once * size, given[1].shape[1]), lambda i, *_: (i, 0)),
            pl.BlockSpec((at_once, size, 2 * size), lambda i, *_: (i, 0, 0)),
        ]
    else:
        in_specs += state_specs
    for _ in pieces:
        if halves:
            in_specs.append(
                pl.BlockSpec((at_once * per, width), lambda i, *_: (jnp.minimum(i, half - 1), 0))
            )
            in_specs.append(pl.BlockSpec((at_once * per, width), lambda i, *_: (jnp.maximum(i - half, 0), 0)))
        else:
            in_specs.append(pl.BlockSpec((at_once * per, width), lambda i, *_: (i, 0)))
    operands = [lengths, shares, q, *given, *flat]
    scratch = [pltpu.VMEM((at_once, count, wide), BF16)]
    if finish:
        value = up_values.shape[2]
        operands.append(up_values)
        in_specs.append(whole)
        out_specs = pl.BlockSpec((total_rows, heads * value), lambda i, *_: (0, 0))
        out_shape = jax.ShapeDtypeStruct((total_rows, heads * value), BF16)
        scratch.append(pltpu.VMEM((heads, total_rows, latent), BF16))
    else:
        out_specs = state_specs
        out_shape = [
            jax.ShapeDtypeStruct((requests, rows, 128), F32),
            jax.ShapeDtypeStruct((requests, rows, 128), F32),
            jax.ShapeDtypeStruct((requests, rows, latent), BF16),
        ]
    return pl.pallas_call(
        functools.partial(attend_kernel, scale, picks, shared, halves, finish),
        grid_spec=pltpu.PrefetchScalarGridSpec(
            num_scalar_prefetch=2,
            grid=(requests // at_once,),
            in_specs=in_specs,
            out_specs=out_specs,
            scratch_shapes=scratch,
        ),
        out_shape=out_shape,
        input_output_aliases={} if shared or finish else {3: 0, 4: 1, 5: 2},
        cost_estimate=pl.CostEstimate(
            flops=2 * requests * rows * count * (2 * latent + 64),
            bytes_accessed=requests * rows * latent * 8,
            transcendentals=requests * rows * count,
        ),
        compiler_params=pltpu.CompilerParams(vmem_limit_bytes=VMEM_LIMIT),
        name=name,
    )(*operands)


def local(
    q_nope,
    q_rope,
    up_keys,
    up_values,
    page_pool,
    page_table,
    lengths,
    prefix_latent,
    tree_latent,
    parents,
):
    heads, nope_dim, latent_dim = up_keys.shape
    rope_dim = q_rope.shape[1] // heads
    scale = (nope_dim + rope_dim) ** (-0.5)
    groups = lax.axis_size("decode")
    shares = lax.axis_size("pool")
    pool_local = page_pool.shape[0]
    width = page_pool.shape[2]
    me = lax.axis_index("pool")

    flat = page_table.reshape(-1)
    entries = flat.shape[0]
    owner_of = flat // pool_local
    order = jnp.arange(entries, dtype=jnp.int32)
    owners = jnp.arange(groups, dtype=jnp.int32) * shares + me
    match = owner_of[None, :] == owners[:, None]
    code = order * pool_local + flat % pool_local
    first = jnp.min(jnp.where(match, code[None, :], entries * pool_local), axis=1)
    last = jnp.max(jnp.where(match, code[None, :], 0), axis=1)
    asks = jnp.stack([first, last], axis=1) % pool_local
    core = me % 2
    prompt = prefix_latent.reshape(-1, 128)
    held = prompt.shape[0] // 2
    prompt = jnp.where(core == 0, prompt[:held], prompt[held:])
    message, held_pool = compose(prompt, asks.astype(BF16), page_pool)
    message = lax.all_to_all(message, "decode", split_axis=0, concat_axis=0, tiled=True)
    wanted = message[:, held, :2].astype(jnp.int32)
    prefix = message[:, :held].reshape(-1, width)
    earlier = (order[None, :] < order[:, None]) & (owner_of[None, :] == owner_of[:, None])
    slot_of = jnp.any(earlier, axis=1).astype(jnp.int32)

    wide = latent_dim + 2 * rope_dim

    packed = pack(wanted, held_pool, shares)
    got = lax.all_to_all(packed, ("decode", "pool"), split_axis=0, concat_axis=0, tiled=True)
    q, hidden = prepare(q_nope, q_rope, up_keys, parents)
    tree = lax.optimization_barrier(jnp.pad(tree_latent, ((0, 0), (0, wide - width))))
    after = hidden[0, :1, :1] + (prefix[:1, :1] + tree[:1, :1]).astype(F32)
    own = compact(owner_of, slot_of, got, after).reshape(-1, 2 * width)

    swap = [(i, i ^ 1) for i in range(shares)]
    up = [(i, (i + 2) % shares) for i in range(shares)]
    down = [(i, (i - 2) % shares) for i in range(shares)]
    me = lax.axis_index("pool")
    other = me + 1 - 2 * (me % 2)
    at = [me, other, me - 2, me + 2, other - 2, other + 2, me + 4, other + 4]
    at = jnp.stack([place % shares for place in at]).astype(jnp.int32)
    def turn(array, pairs):
        return lax.ppermute(array, "pool", pairs)

    def call(name, picks, given, pieces, **more):
        return attend(
            name, scale, lengths, at, picks, q, name == "first", given, pieces, **more
        )

    below = turn(own, up)
    above = turn(own, down)
    beside = turn(own, swap)
    beside, prefix = lax.optimization_barrier((beside, prefix))
    prefix = jnp.concatenate([prefix, turn(prefix, swap)], axis=0)
    prefix = jnp.pad(prefix, ((0, 0), (0, wide - width)))
    state = call("first", (0, 1), (prefix, tree, hidden), [own, beside], at_once=2)
    below, above, state = lax.optimization_barrier((below, above, state))
    middle = own.shape[0] // 2
    far_low = turn(below[:middle], up)
    far_high = turn(above[middle:], down)
    state = call(
        "second",
        (2, 3, 4, 5),
        state,
        [below, above, turn(below, swap), turn(above, swap)],
        at_once=2,
    )
    far_low, far_high, state = lax.optimization_barrier((far_low, far_high, state))
    return call(
        "third",
        (6, 7),
        state,
        [(far_low, far_high), (turn(far_low, swap), turn(far_high, swap))],
        up_values=up_values,
        at_once=4,
    )


def solution(mesh):
    in_specs = (
        P("decode", "pool"),
        P("decode", "pool"),
        P("pool", None, None),
        P("pool", None, None),
        P(("decode", "pool"), None, None),
        P("decode", None),
        P("decode"),
        P("decode", None),
        P("decode", None),
        P("decode", None),
    )
    out_specs = P("decode", "pool")
    return jax.shard_map(local, mesh=mesh, in_specs=in_specs, out_specs=out_specs, check_vma=False)
```

```python
import functools
import math

import jax
import jax.numpy as jnp
from jax import lax
from jax.experimental import pallas as pl
from jax.experimental.pallas import tpu as pltpu
from jax.sharding import PartitionSpec as P

F32 = jnp.float32
BF16 = jnp.bfloat16
VMEM_LIMIT = 24 * 1024 * 1024


def nt_dot(a, b):
    return lax.dot_general(a, b, (((1,), (1,)), ((), ())), preferred_element_type=F32)


def prepare_kernel(rows_ref, rope_ref, keys_ref, parents_ref, q_ref, seen_ref):
    head = pl.program_id(0)
    latent = keys_ref.shape[2]
    absorbed = jnp.dot(rows_ref[...], keys_ref[0], preferred_element_type=F32)
    q_ref[0, :, :latent] = absorbed.astype(BF16)
    pair = rope_ref[...].astype(F32)
    lane = lax.broadcasted_iota(jnp.int32, pair.shape, 1)
    half = pair.shape[1] // 2
    turned = pltpu.roll(pair, half, 1)
    even = lax.rem(head, 2) == 0
    source = jnp.where(even, pair, turned)
    other = jnp.where(even, turned, pair)
    q_ref[0, :, latent : latent + 2 * half] = jnp.where(lane < half, source, 0.0).astype(BF16)
    q_ref[0, :, latent + 2 * half :] = jnp.where(lane >= half, other, 0.0).astype(BF16)
    size = parents_ref.shape[1]
    columns = lax.broadcasted_iota(jnp.int32, (size, size), 1)
    rows = lax.broadcasted_iota(jnp.int32, (size, size), 0)
    links = (parents_ref[0] == columns) | (rows == columns)
    reach = links.astype(F32)
    for sweep in range(max(1, (size - 1).bit_length())):
        reach = jnp.minimum(
            jnp.dot(reach.astype(BF16), reach.astype(BF16), preferred_element_type=F32), 1.0
        )
    lowest = jnp.full((size, size), -jnp.inf, F32)
    seen_ref[0] = jnp.concatenate([jnp.where(reach > 0.5, 0.0, lowest), lowest], axis=1)


def prepare(q_nope, q_rope, up_keys, parents):
    heads, nope, latent = up_keys.shape
    rows = q_nope.shape[0]
    requests, size = parents.shape
    rope = q_rope.shape[1] // heads
    return pl.pallas_call(
        prepare_kernel,
        grid=(heads,),
        in_specs=[
            pl.BlockSpec((rows, nope), lambda h: (0, h)),
            pl.BlockSpec((rows, 2 * rope), lambda h: (0, h // 2)),
            pl.BlockSpec((1, nope, latent), lambda h: (h, 0, 0)),
            pl.BlockSpec((1, size, 1), lambda h: (h, 0, 0)),
        ],
        out_specs=[
            pl.BlockSpec((1, rows, latent + 4 * rope), lambda h: (h, 0, 0)),
            pl.BlockSpec((1, size, 2 * size), lambda h: (h, 0, 0)),
        ],
        out_shape=[
            jax.ShapeDtypeStruct((heads, rows, latent + 4 * rope), BF16),
            jax.ShapeDtypeStruct((requests, size, 2 * size), F32),
        ],
        cost_estimate=pl.CostEstimate(
            flops=2 * rows * heads * nope * latent, bytes_accessed=10_000_000, transcendentals=0
        ),
        compiler_params=pltpu.CompilerParams(vmem_limit_bytes=VMEM_LIMIT),
        name="prepare",
    )(q_nope, q_rope, up_keys, parents[:, :, None])


def compose_kernel(held, prompt_ref, asks_ref, pool_ref, out_ref, pool_out_ref):
    prompt = prompt_ref[...].astype(F32)
    asks = asks_ref[...].astype(F32)
    rows = lax.broadcasted_iota(jnp.int32, prompt.shape, 0)
    for group in range(out_ref.shape[0]):
        out_ref[group] = jnp.where(rows == held, asks[group : group + 1, :], prompt).astype(BF16)


def compose(prompt, asks, pool):
    held = prompt.shape[0]
    rows = held + 16 - held % 16
    prompt = jnp.pad(prompt, ((0, rows - held), (0, 0)))
    asks = jnp.pad(asks, ((0, 0), (0, 126)))
    return pl.pallas_call(
        functools.partial(compose_kernel, held),
        in_specs=[pl.BlockSpec(memory_space=pltpu.VMEM)] * 3,
        out_specs=[pl.BlockSpec(memory_space=pltpu.VMEM)] * 2,
        out_shape=[
            jax.ShapeDtypeStruct((asks.shape[0], rows, 128), BF16),
            jax.ShapeDtypeStruct(pool.shape, pool.dtype),
        ],
        input_output_aliases={2: 1},
        cost_estimate=pl.CostEstimate(flops=0, bytes_accessed=1_000_000, transcendentals=0),
        compiler_params=pltpu.CompilerParams(vmem_limit_bytes=VMEM_LIMIT),
        name="compose",
    )(prompt, asks, pool)


def pack_kernel(wanted_ref, pool_ref, out_ref):
    size = pool_ref.shape[1]
    some = out_ref.shape[0] // size
    latent = 512
    for index in range(some):
        group = pl.program_id(0) * some + index
        first = pool_ref.at[wanted_ref[group, 0]]
        second = pool_ref.at[wanted_ref[group, 1]]
        rows = slice(index * size, (index + 1) * size)
        out_ref[rows, :latent] = first[:, :latent]
        out_ref[rows, latent : 2 * latent] = second[:, :latent]
        out_ref[rows, 2 * latent :] = jnp.concatenate(
            [first[:, latent:], second[:, latent:]], axis=1
        )


def pack(wanted, pool, shares):
    groups = wanted.shape[0]
    size, width = pool.shape[1:]
    steps = 4
    packed = pl.pallas_call(
        pack_kernel,
        grid=(steps,),
        in_specs=[
            pl.BlockSpec(memory_space=pltpu.SMEM),
            pl.BlockSpec(memory_space=pltpu.VMEM),
        ],
        out_specs=pl.BlockSpec((groups // steps * size, 2 * width), lambda i: (i, 0)),
        out_shape=pltpu.HBM((groups * size, 2 * width), BF16),
        cost_estimate=pl.CostEstimate(flops=0, bytes_accessed=5_000_000, transcendentals=0),
        compiler_params=pltpu.CompilerParams(vmem_limit_bytes=VMEM_LIMIT),
        name="pack",
    )(wanted, pool)
    return packed.reshape(groups * shares, size // shares, 2 * width)


def compact_kernel(source_ref, slot_ref, got_ref, after_ref, out_ref):
    pairs = out_ref.shape[0]
    per = 8
    latent = 512
    half = (out_ref.shape[2] - 2 * latent) // 2

    def body(k, carry):
        request = k // per
        first = request * (2 * per) + lax.rem(k, per)
        ropes = []
        for side, entry in enumerate((first, first + per)):
            source = source_ref[entry]
            slot = slot_ref[entry]
            start = pl.multiple_of(slot * latent, latent)
            out_ref[k, :, side * latent : (side + 1) * latent] = got_ref[
                source, :, pl.ds(start, latent)
            ]
            both = got_ref[source, :, 2 * latent :].astype(F32)
            ropes.append(jnp.where(slot == side, both, pltpu.roll(both, half, 1)))
        lane = lax.broadcasted_iota(jnp.int32, ropes[0].shape, 1)
        out_ref[k, :, 2 * latent :] = jnp.where(lane < half, ropes[0], ropes[1]).astype(BF16)
        return carry

    lax.fori_loop(0, pairs, body, 0, unroll=4)


def compact(source, slot, got, after):
    entries = source.shape[0]
    return pl.pallas_call(
        compact_kernel,
        in_specs=[
            pl.BlockSpec(memory_space=pltpu.SMEM),
            pl.BlockSpec(memory_space=pltpu.SMEM),
            pl.BlockSpec(memory_space=pltpu.VMEM),
            pl.BlockSpec(memory_space=pltpu.SMEM),
        ],
        out_specs=pl.BlockSpec(memory_space=pltpu.VMEM),
        out_shape=jax.ShapeDtypeStruct((entries // 2,) + got.shape[1:], BF16),
        cost_estimate=pl.CostEstimate(flops=0, bytes_accessed=4_000_000, transcendentals=0),
        compiler_params=pltpu.CompilerParams(vmem_limit_bytes=VMEM_LIMIT),
        name="compact",
    )(source, slot, got, after)


def spread(column, width):
    if width <= 128:
        return column[:, :width]
    return jnp.concatenate([column] * (width // 128), axis=1)


def attend_kernel(scale, picks, shared, halves, finish, lengths_ref, shares_ref, q_ref, *refs):
    refs = list(refs)
    taken = [refs.pop(0) for _ in range(3)]
    pieces = [
        (refs.pop(0), refs.pop(0)) if halves else (refs.pop(0),) for _ in range(len(picks))
    ]
    values_ref = refs.pop(0) if finish else None
    if finish:
        out_ref, keys_ref, mixed_ref = refs
    else:
        top_out, total_out, sum_out, keys_ref = refs
    heads, total_rows, wide = q_ref.shape
    size = total_rows // lengths_ref.shape[0]
    latent = wide - 256
    whole = halves and keys_ref.shape[0] == lengths_ref.shape[0]
    part = pieces[0][0].shape[0] // 2 // keys_ref.shape[0] * (2 if whole else 1)
    section = len(picks) * part
    origin = keys_ref.shape[1] - 4 * section
    step_requests = keys_ref.shape[0]
    factor = scale * math.log2(math.e)
    lowest = F32(-jnp.inf)
    some = 8
    block = some * size

    @pl.when(pl.program_id(0) == 0)
    def _():
        for turn in range(step_requests):
            keys_ref[turn, :, latent:] = jnp.zeros((keys_ref.shape[1], 256), BF16)
            if shared:
                prompt = taken[0].shape[0]
                keys_ref[turn, :prompt, : latent + 128] = taken[0][...]
                keys_ref[turn, prompt + size : origin, :latent] = jnp.zeros(
                    (origin - prompt - size, latent), BF16
                )

    for turn in range(step_requests):
        if shared:
            prompt = taken[0].shape[0]
            keys_ref[turn, prompt : prompt + size, : latent + 128] = taken[1][turn * size : (turn + 1) * size]
        for which, refs_of in enumerate(pieces):
            half_of, place = divmod(turn, step_requests // 2) if whole else (0, turn)
            piece = refs_of[half_of][place * 2 * part : (place + 1) * 2 * part]
            if halves and not whole:
                piece = jnp.where(pl.program_id(0) < pl.num_programs(0) // 2, piece, refs_of[1][turn * 2 * part : (turn + 1) * 2 * part])
            for index in range(4):
                side, half = index // 2, index % 2
                rows = slice(
                    origin + index * section + which * part,
                    origin + index * section + (which + 1) * part,
                )
                some_rows = piece[half * part : (half + 1) * part]
                keys_ref[turn, rows, :latent] = some_rows[:, side * latent : (side + 1) * latent]
                keys_ref[turn, rows, latent + side * 128 : latent + (side + 1) * 128] = some_rows[
                    :, 2 * latent :
                ]

    def work(turn, request, length, sections):
        count = sections * section
        column = lax.broadcasted_iota(jnp.int32, (1, count), 1)
        position = column // section * 256 + column % part // 8 * 64 + column % 8
        for which, pick in enumerate(picks):
            position = position + jnp.where(
                column // part % len(picks) == which, shares_ref[pick] * 8, 0
            )
        bias = jnp.where(position < length, 0.0, lowest)
        if shared:
            hidden = jnp.concatenate([taken[2][turn]] * some, axis=0)
        for step in range(heads // some):
            which = slice(step * some, (step + 1) * some)
            rows = slice(step * block, (step + 1) * block)
            q = q_ref[which, pl.ds(pl.multiple_of(request * size, size), size), :]
            q = q.reshape(block, wide)
            scores = nt_dot(q, keys_ref[turn, origin : origin + count, :]) + bias
            if shared:
                first = nt_dot(q, keys_ref[turn, :prompt, :])
                tree = nt_dot(q, keys_ref[turn, prompt:origin, :]) + hidden
                scores = jnp.concatenate([first, tree, scores], axis=1)
            top = jnp.broadcast_to(jnp.max(scores, axis=1, keepdims=True), (block, 128))
            if not shared:
                before = taken[0][request, rows, :]
                top = jnp.maximum(top, before)
                fade = jnp.exp2((before - top) * factor)
            weights = jnp.exp2((scores - spread(top, scores.shape[1])) * factor)
            if finish:
                weights = weights.astype(BF16)
                ones = jnp.ones((weights.shape[1], 128), BF16)
                total = jnp.dot(weights, ones, preferred_element_type=F32)
            else:
                total = jnp.broadcast_to(jnp.sum(weights, axis=1, keepdims=True), (block, 128))
            mixed = jnp.dot(
                weights.astype(BF16),
                keys_ref[turn, 0 if shared else origin : origin + count, :latent],
                preferred_element_type=F32,
            )
            if not shared:
                total = total + taken[1][request, rows, :] * fade
                mixed = mixed + taken[2][request, rows, :].astype(F32) * spread(fade, latent)
            if finish:
                mixed = mixed * spread(1.0 / total, latent)
                mixed_ref[which, pl.ds(pl.multiple_of(request * size, size), size), :] = (
                    mixed.astype(BF16).reshape(some, size, latent)
                )
            else:
                top_out[request, rows, :] = top
                total_out[request, rows, :] = total
                sum_out[request, rows, :] = mixed.astype(BF16)

    steps = (4,) if step_requests > 1 else (1, 2, 3, 4) if section % 128 == 0 else (2, 4)
    for turn in range(step_requests):
        request = pl.program_id(0) * step_requests + turn
        length = lengths_ref[request]
        needed = pl.cdiv(length, 256)
        if len(steps) == 1:
            work(turn, request, length, steps[0])
        else:
            for low, high in zip((0,) + steps, steps):

                @pl.when((needed > low) & (needed <= high))
                def _():
                    work(turn, request, length, high)

    if finish:
        value = values_ref.shape[2]

        @pl.when(pl.program_id(0) == pl.num_programs(0) - 1)
        def _():
            for head in range(heads):
                out_ref[:, head * value : (head + 1) * value] = jnp.dot(
                    mixed_ref[head], values_ref[head], preferred_element_type=F32
                ).astype(BF16)


def attend(name, scale, lengths, shares, picks, q, shared, given, pieces, up_values=None, at_once=1):
    heads, total_rows, wide = q.shape
    requests = lengths.shape[0]
    size = total_rows // requests
    rows = heads * size
    latent = wide - 256
    halves = isinstance(pieces[0], tuple)
    finish = up_values is not None
    flat = [array for piece in pieces for array in (piece if halves else (piece,))]
    per = flat[0].shape[0] * (2 if halves else 1) // requests
    width = flat[0].shape[1]
    half = requests // 2 // at_once
    origin = given[0].shape[0] + 2 * size if shared else 0
    count = origin + 2 * per * len(pieces)

    whole = pl.BlockSpec(memory_space=pltpu.VMEM)
    state_specs = [whole, whole, whole]
    in_specs = [whole]
    if shared:
        in_specs += [
            pl.BlockSpec(given[0].shape, lambda i, *_: (0, 0)),
            pl.BlockSpec((at_once * size, given[1].shape[1]), lambda i, *_: (i, 0)),
            pl.BlockSpec((at_once, size, 2 * size), lambda i, *_: (i, 0, 0)),
        ]
    else:
        in_specs += state_specs
    for _ in pieces:
        if halves and half == 0:
            in_specs += [whole, whole]
        elif halves:
            in_specs.append(
                pl.BlockSpec((at_once * per, width), lambda i, *_: (jnp.minimum(i, half - 1), 0))
            )
            in_specs.append(pl.BlockSpec((at_once * per, width), lambda i, *_: (jnp.maximum(i - half, 0), 0)))
        else:
            in_specs.append(pl.BlockSpec((at_once * per, width), lambda i, *_: (i, 0)))
    operands = [lengths, shares, q, *given, *flat]
    scratch = [pltpu.VMEM((at_once, count, wide), BF16)]
    if finish:
        value = up_values.shape[2]
        operands.append(up_values)
        in_specs.append(whole)
        out_specs = pl.BlockSpec((total_rows, heads * value), lambda i, *_: (0, 0))
        out_shape = jax.ShapeDtypeStruct((total_rows, heads * value), BF16)
        scratch.append(pltpu.VMEM((heads, total_rows, latent), BF16))
    else:
        out_specs = state_specs
        out_shape = [
            jax.ShapeDtypeStruct((requests, rows, 128), F32),
            jax.ShapeDtypeStruct((requests, rows, 128), F32),
            jax.ShapeDtypeStruct((requests, rows, latent), BF16),
        ]
    return pl.pallas_call(
        functools.partial(attend_kernel, scale, picks, shared, halves, finish),
        grid_spec=pltpu.PrefetchScalarGridSpec(
            num_scalar_prefetch=2,
            grid=(requests // at_once,),
            in_specs=in_specs,
            out_specs=out_specs,
            scratch_shapes=scratch,
        ),
        out_shape=out_shape,
        input_output_aliases={} if shared or finish else {3: 0, 4: 1, 5: 2},
        cost_estimate=pl.CostEstimate(
            flops=2 * requests * rows * count * (2 * latent + 64),
            bytes_accessed=requests * rows * latent * 8,
            transcendentals=requests * rows * count,
        ),
        compiler_params=pltpu.CompilerParams(vmem_limit_bytes=VMEM_LIMIT),
        name=name,
    )(*operands)


def local(
    q_nope,
    q_rope,
    up_keys,
    up_values,
    page_pool,
    page_table,
    lengths,
    prefix_latent,
    tree_latent,
    parents,
):
    heads, nope_dim, latent_dim = up_keys.shape
    rope_dim = q_rope.shape[1] // heads
    scale = (nope_dim + rope_dim) ** (-0.5)
    groups = lax.axis_size("decode")
    shares = lax.axis_size("pool")
    pool_local = page_pool.shape[0]
    width = page_pool.shape[2]
    me = lax.axis_index("pool")

    flat = page_table.reshape(-1)
    entries = flat.shape[0]
    owner_of = flat // pool_local
    order = jnp.arange(entries, dtype=jnp.int32)
    owners = jnp.arange(groups, dtype=jnp.int32) * shares + me
    match = owner_of[None, :] == owners[:, None]
    code = order * pool_local + flat % pool_local
    first = jnp.min(jnp.where(match, code[None, :], entries * pool_local), axis=1)
    last = jnp.max(jnp.where(match, code[None, :], 0), axis=1)
    asks = jnp.stack([first, last], axis=1) % pool_local
    core = me % 2
    prompt = prefix_latent.reshape(-1, 128)
    held = prompt.shape[0] // 2
    prompt = jnp.where(core == 0, prompt[:held], prompt[held:])
    message, held_pool = compose(prompt, asks.astype(BF16), page_pool)
    message = lax.all_to_all(message, "decode", split_axis=0, concat_axis=0, tiled=True)
    wanted = message[:, held, :2].astype(jnp.int32)
    prefix = message[:, :held].reshape(-1, width)
    earlier = (order[None, :] < order[:, None]) & (owner_of[None, :] == owner_of[:, None])
    slot_of = jnp.any(earlier, axis=1).astype(jnp.int32)

    wide = latent_dim + 2 * rope_dim

    packed = pack(wanted, held_pool, shares)
    got = lax.all_to_all(packed, ("decode", "pool"), split_axis=0, concat_axis=0, tiled=True)
    q, hidden = prepare(q_nope, q_rope, up_keys, parents)
    tree = lax.optimization_barrier(jnp.pad(tree_latent, ((0, 0), (0, wide - width))))
    after = hidden[0, :1, :1] + (prefix[:1, :1] + tree[:1, :1]).astype(F32)
    own = compact(owner_of, slot_of, got, after).reshape(-1, 2 * width)

    swap = [(i, i ^ 1) for i in range(shares)]
    up = [(i, (i + 2) % shares) for i in range(shares)]
    down = [(i, (i - 2) % shares) for i in range(shares)]
    me = lax.axis_index("pool")
    other = me + 1 - 2 * (me % 2)
    at = [me, other, me - 2, me + 2, other - 2, other + 2, me + 4, other + 4]
    at = jnp.stack([place % shares for place in at]).astype(jnp.int32)
    def turn(array, pairs):
        return lax.ppermute(array, "pool", pairs)

    def call(name, picks, given, pieces, **more):
        return attend(
            name, scale, lengths, at, picks, q, name == "first", given, pieces, **more
        )

    below = turn(own, up)
    above = turn(own, down)
    beside = turn(own, swap)
    beside, prefix = lax.optimization_barrier((beside, prefix))
    prefix = jnp.concatenate([prefix, turn(prefix, swap)], axis=0)
    prefix = jnp.pad(prefix, ((0, 0), (0, wide - width)))
    state = call("first", (0, 1), (prefix, tree, hidden), [own, beside], at_once=2)
    below, above, state = lax.optimization_barrier((below, above, state))
    middle = own.shape[0] // 2
    far_low = turn(below[:middle], up)
    far_high = turn(above[middle:], down)
    state = call(
        "second",
        (2, 3, 4, 5),
        state,
        [below, above, turn(below, swap), turn(above, swap)],
        at_once=2,
    )
    far_low, far_high, state = lax.optimization_barrier((far_low, far_high, state))
    return call(
        "third",
        (6, 7),
        state,
        [(far_low, far_high), (turn(far_low, swap), turn(far_high, swap))],
        up_values=up_values,
        at_once=8,
    )


def solution(mesh):
    in_specs = (
        P("decode", "pool"),
        P("decode", "pool"),
        P("pool", None, None),
        P("pool", None, None),
        P(("decode", "pool"), None, None),
        P("decode", None),
        P("decode"),
        P("decode", None),
        P("decode", None),
        P("decode", None),
    )
    out_specs = P("decode", "pool")
    return jax.shard_map(local, mesh=mesh, in_specs=in_specs, out_specs=out_specs, check_vma=False)
```

```python
import functools
import math

import jax
import jax.numpy as jnp
from jax import lax
from jax.experimental import pallas as pl
from jax.experimental.pallas import tpu as pltpu
from jax.sharding import PartitionSpec as P

F32 = jnp.float32
BF16 = jnp.bfloat16
VMEM_LIMIT = 24 * 1024 * 1024


def nt_dot(a, b):
    return lax.dot_general(a, b, (((1,), (1,)), ((), ())), preferred_element_type=F32)


def prepare_kernel(rows_ref, rope_ref, keys_ref, parents_ref, q_ref, seen_ref):
    head = pl.program_id(0)
    latent = keys_ref.shape[2]
    absorbed = jnp.dot(rows_ref[...], keys_ref[0], preferred_element_type=F32)
    q_ref[0, :, :latent] = absorbed.astype(BF16)
    pair = rope_ref[...].astype(F32)
    lane = lax.broadcasted_iota(jnp.int32, pair.shape, 1)
    half = pair.shape[1] // 2
    turned = pltpu.roll(pair, half, 1)
    even = lax.rem(head, 2) == 0
    source = jnp.where(even, pair, turned)
    other = jnp.where(even, turned, pair)
    q_ref[0, :, latent : latent + 2 * half] = jnp.where(lane < half, source, 0.0).astype(BF16)
    q_ref[0, :, latent + 2 * half :] = jnp.where(lane >= half, other, 0.0).astype(BF16)
    size = parents_ref.shape[1]
    columns = lax.broadcasted_iota(jnp.int32, (size, size), 1)
    rows = lax.broadcasted_iota(jnp.int32, (size, size), 0)
    links = (parents_ref[0] == columns) | (rows == columns)
    reach = links.astype(F32)
    for sweep in range(max(1, (size - 1).bit_length())):
        reach = jnp.minimum(
            jnp.dot(reach.astype(BF16), reach.astype(BF16), preferred_element_type=F32), 1.0
        )
    lowest = jnp.full((size, size), -jnp.inf, F32)
    seen_ref[0] = jnp.concatenate([jnp.where(reach > 0.5, 0.0, lowest), lowest], axis=1)


def prepare(q_nope, q_rope, up_keys, parents):
    heads, nope, latent = up_keys.shape
    rows = q_nope.shape[0]
    requests, size = parents.shape
    rope = q_rope.shape[1] // heads
    return pl.pallas_call(
        prepare_kernel,
        grid=(heads,),
        in_specs=[
            pl.BlockSpec((rows, nope), lambda h: (0, h)),
            pl.BlockSpec((rows, 2 * rope), lambda h: (0, h // 2)),
            pl.BlockSpec((1, nope, latent), lambda h: (h, 0, 0)),
            pl.BlockSpec((1, size, 1), lambda h: (h, 0, 0)),
        ],
        out_specs=[
            pl.BlockSpec((1, rows, latent + 4 * rope), lambda h: (h, 0, 0)),
            pl.BlockSpec((1, size, 2 * size), lambda h: (h, 0, 0)),
        ],
        out_shape=[
            jax.ShapeDtypeStruct((heads, rows, latent + 4 * rope), BF16),
            jax.ShapeDtypeStruct((requests, size, 2 * size), F32),
        ],
        cost_estimate=pl.CostEstimate(
            flops=2 * rows * heads * nope * latent, bytes_accessed=10_000_000, transcendentals=0
        ),
        compiler_params=pltpu.CompilerParams(vmem_limit_bytes=VMEM_LIMIT),
        name="prepare",
    )(q_nope, q_rope, up_keys, parents[:, :, None])


def compose_kernel(held, prompt_ref, asks_ref, pool_ref, out_ref, pool_out_ref):
    prompt = prompt_ref[...].astype(F32)
    asks = asks_ref[...].astype(F32)
    rows = lax.broadcasted_iota(jnp.int32, prompt.shape, 0)
    for group in range(out_ref.shape[0]):
        out_ref[group] = jnp.where(rows == held, asks[group : group + 1, :], prompt).astype(BF16)


def compose(prompt, asks, pool):
    held = prompt.shape[0]
    rows = held + 16 - held % 16
    prompt = jnp.pad(prompt, ((0, rows - held), (0, 0)))
    asks = jnp.pad(asks, ((0, 0), (0, 126)))
    return pl.pallas_call(
        functools.partial(compose_kernel, held),
        in_specs=[pl.BlockSpec(memory_space=pltpu.VMEM)] * 3,
        out_specs=[pl.BlockSpec(memory_space=pltpu.VMEM)] * 2,
        out_shape=[
            jax.ShapeDtypeStruct((asks.shape[0], rows, 128), BF16),
            jax.ShapeDtypeStruct(pool.shape, pool.dtype),
        ],
        input_output_aliases={2: 1},
        cost_estimate=pl.CostEstimate(flops=0, bytes_accessed=1_000_000, transcendentals=0),
        compiler_params=pltpu.CompilerParams(vmem_limit_bytes=VMEM_LIMIT),
        name="compose",
    )(prompt, asks, pool)


def pack_kernel(wanted_ref, pool_ref, out_ref):
    size = pool_ref.shape[1]
    some = out_ref.shape[0] // size
    latent = 512
    for index in range(some):
        group = pl.program_id(0) * some + index
        first = pool_ref.at[wanted_ref[group, 0]]
        second = pool_ref.at[wanted_ref[group, 1]]
        rows = slice(index * size, (index + 1) * size)
        out_ref[rows, :latent] = first[:, :latent]
        out_ref[rows, latent : 2 * latent] = second[:, :latent]
        out_ref[rows, 2 * latent :] = jnp.concatenate(
            [first[:, latent:], second[:, latent:]], axis=1
        )


def pack(wanted, pool, shares):
    groups = wanted.shape[0]
    size, width = pool.shape[1:]
    steps = 2
    packed = pl.pallas_call(
        pack_kernel,
        grid=(steps,),
        in_specs=[
            pl.BlockSpec(memory_space=pltpu.SMEM),
            pl.BlockSpec(memory_space=pltpu.VMEM),
        ],
        out_specs=pl.BlockSpec((groups // steps * size, 2 * width), lambda i: (i, 0)),
        out_shape=pltpu.HBM((groups * size, 2 * width), BF16),
        cost_estimate=pl.CostEstimate(flops=0, bytes_accessed=5_000_000, transcendentals=0),
        compiler_params=pltpu.CompilerParams(vmem_limit_bytes=VMEM_LIMIT),
        name="pack",
    )(wanted, pool)
    return packed.reshape(groups * shares, size // shares, 2 * width)


def compact_kernel(source_ref, slot_ref, got_ref, after_ref, out_ref):
    pairs = out_ref.shape[0]
    per = 8
    latent = 512
    half = (out_ref.shape[2] - 2 * latent) // 2

    def body(k, carry):
        request = k // per
        first = request * (2 * per) + lax.rem(k, per)
        ropes = []
        for side, entry in enumerate((first, first + per)):
            source = source_ref[entry]
            slot = slot_ref[entry]
            start = pl.multiple_of(slot * latent, latent)
            out_ref[k, :, side * latent : (side + 1) * latent] = got_ref[
                source, :, pl.ds(start, latent)
            ]
            both = got_ref[source, :, 2 * latent :].astype(F32)
            ropes.append(jnp.where(slot == side, both, pltpu.roll(both, half, 1)))
        lane = lax.broadcasted_iota(jnp.int32, ropes[0].shape, 1)
        out_ref[k, :, 2 * latent :] = jnp.where(lane < half, ropes[0], ropes[1]).astype(BF16)
        return carry

    lax.fori_loop(0, pairs, body, 0, unroll=16)


def compact(source, slot, got, after):
    entries = source.shape[0]
    return pl.pallas_call(
        compact_kernel,
        in_specs=[
            pl.BlockSpec(memory_space=pltpu.SMEM),
            pl.BlockSpec(memory_space=pltpu.SMEM),
            pl.BlockSpec(memory_space=pltpu.VMEM),
            pl.BlockSpec(memory_space=pltpu.SMEM),
        ],
        out_specs=pl.BlockSpec(memory_space=pltpu.VMEM),
        out_shape=jax.ShapeDtypeStruct((entries // 2,) + got.shape[1:], BF16),
        cost_estimate=pl.CostEstimate(flops=0, bytes_accessed=4_000_000, transcendentals=0),
        compiler_params=pltpu.CompilerParams(vmem_limit_bytes=VMEM_LIMIT),
        name="compact",
    )(source, slot, got, after)


def spread(column, width):
    if width <= 128:
        return column[:, :width]
    return jnp.concatenate([column] * (width // 128), axis=1)


def attend_kernel(scale, picks, shared, halves, finish, lengths_ref, shares_ref, q_ref, *refs):
    refs = list(refs)
    taken = [refs.pop(0) for _ in range(3)]
    pieces = [
        (refs.pop(0), refs.pop(0)) if halves else (refs.pop(0),) for _ in range(len(picks))
    ]
    values_ref = refs.pop(0) if finish else None
    if finish:
        out_ref, keys_ref, mixed_ref = refs
    else:
        top_out, total_out, sum_out, keys_ref = refs
    heads, total_rows, wide = q_ref.shape
    size = total_rows // lengths_ref.shape[0]
    latent = wide - 256
    whole = halves and keys_ref.shape[0] == lengths_ref.shape[0]
    part = pieces[0][0].shape[0] // 2 // keys_ref.shape[0] * (2 if whole else 1)
    section = len(picks) * part
    origin = keys_ref.shape[1] - 4 * section
    step_requests = keys_ref.shape[0]
    factor = scale * math.log2(math.e)
    lowest = F32(-jnp.inf)
    some = 8
    block = some * size

    @pl.when(pl.program_id(0) == 0)
    def _():
        for turn in range(step_requests):
            keys_ref[turn, :, latent:] = jnp.zeros((keys_ref.shape[1], 256), BF16)
            if shared:
                prompt = taken[0].shape[0]
                keys_ref[turn, :prompt, : latent + 128] = taken[0][...]
                keys_ref[turn, prompt + size : origin, :latent] = jnp.zeros(
                    (origin - prompt - size, latent), BF16
                )

    for turn in range(step_requests):
        if shared:
            prompt = taken[0].shape[0]
            keys_ref[turn, prompt : prompt + size, : latent + 128] = taken[1][turn * size : (turn + 1) * size]
        for which, refs_of in enumerate(pieces):
            half_of, place = divmod(turn, step_requests // 2) if whole else (0, turn)
            piece = refs_of[half_of][place * 2 * part : (place + 1) * 2 * part]
            if halves and not whole:
                piece = jnp.where(pl.program_id(0) < pl.num_programs(0) // 2, piece, refs_of[1][turn * 2 * part : (turn + 1) * 2 * part])
            for index in range(4):
                side, half = index // 2, index % 2
                rows = slice(
                    origin + index * section + which * part,
                    origin + index * section + (which + 1) * part,
                )
                some_rows = piece[half * part : (half + 1) * part]
                keys_ref[turn, rows, :latent] = some_rows[:, side * latent : (side + 1) * latent]
                keys_ref[turn, rows, latent + side * 128 : latent + (side + 1) * 128] = some_rows[
                    :, 2 * latent :
                ]

    def work(turn, request, length, sections):
        count = sections * section
        column = lax.broadcasted_iota(jnp.int32, (1, count), 1)
        position = column // section * 256 + column % part // 8 * 64 + column % 8
        for which, pick in enumerate(picks):
            position = position + jnp.where(
                column // part % len(picks) == which, shares_ref[pick] * 8, 0
            )
        bias = jnp.where(position < length, 0.0, lowest)
        if shared:
            hidden = jnp.concatenate([taken[2][turn]] * some, axis=0)
        for step in range(heads // some):
            which = slice(step * some, (step + 1) * some)
            rows = slice(step * block, (step + 1) * block)
            q = q_ref[which, pl.ds(pl.multiple_of(request * size, size), size), :]
            q = q.reshape(block, wide)
            scores = nt_dot(q, keys_ref[turn, origin : origin + count, :]) + bias
            if shared:
                first = nt_dot(q, keys_ref[turn, :prompt, :])
                tree = nt_dot(q, keys_ref[turn, prompt:origin, :]) + hidden
                scores = jnp.concatenate([first, tree, scores], axis=1)
            top = jnp.broadcast_to(jnp.max(scores, axis=1, keepdims=True), (block, 128))
            if not shared:
                before = taken[0][request, rows, :]
                top = jnp.maximum(top, before)
                fade = jnp.exp2((before - top) * factor)
            weights = jnp.exp2((scores - spread(top, scores.shape[1])) * factor)
            if finish:
                weights = weights.astype(BF16)
                ones = jnp.ones((weights.shape[1], 128), BF16)
                total = jnp.dot(weights, ones, preferred_element_type=F32)
            else:
                total = jnp.broadcast_to(jnp.sum(weights, axis=1, keepdims=True), (block, 128))
            mixed = jnp.dot(
                weights.astype(BF16),
                keys_ref[turn, 0 if shared else origin : origin + count, :latent],
                preferred_element_type=F32,
            )
            if not shared:
                total = total + taken[1][request, rows, :] * fade
                mixed = mixed + taken[2][request, rows, :].astype(F32) * spread(fade, latent)
            if finish:
                mixed = mixed * spread(1.0 / total, latent)
                mixed_ref[which, pl.ds(pl.multiple_of(request * size, size), size), :] = (
                    mixed.astype(BF16).reshape(some, size, latent)
                )
            else:
                top_out[request, rows, :] = top
                total_out[request, rows, :] = total
                sum_out[request, rows, :] = mixed.astype(BF16)

    steps = (4,) if step_requests > 1 else (1, 2, 3, 4) if section % 128 == 0 else (2, 4)
    for turn in range(step_requests):
        request = pl.program_id(0) * step_requests + turn
        length = lengths_ref[request]
        needed = pl.cdiv(length, 256)
        if len(steps) == 1:
            work(turn, request, length, steps[0])
        else:
            for low, high in zip((0,) + steps, steps):

                @pl.when((needed > low) & (needed <= high))
                def _():
                    work(turn, request, length, high)

    if finish:
        value = values_ref.shape[2]

        @pl.when(pl.program_id(0) == pl.num_programs(0) - 1)
        def _():
            for head in range(heads):
                out_ref[:, head * value : (head + 1) * value] = jnp.dot(
                    mixed_ref[head], values_ref[head], preferred_element_type=F32
                ).astype(BF16)


def attend(name, scale, lengths, shares, picks, q, shared, given, pieces, up_values=None, at_once=1):
    heads, total_rows, wide = q.shape
    requests = lengths.shape[0]
    size = total_rows // requests
    rows = heads * size
    latent = wide - 256
    halves = isinstance(pieces[0], tuple)
    finish = up_values is not None
    flat = [array for piece in pieces for array in (piece if halves else (piece,))]
    per = flat[0].shape[0] * (2 if halves else 1) // requests
    width = flat[0].shape[1]
    half = requests // 2 // at_once
    origin = given[0].shape[0] + 2 * size if shared else 0
    count = origin + 2 * per * len(pieces)

    whole = pl.BlockSpec(memory_space=pltpu.VMEM)
    state_specs = [whole, whole, whole]
    in_specs = [whole]
    if shared:
        in_specs += [
            pl.BlockSpec(given[0].shape, lambda i, *_: (0, 0)),
            pl.BlockSpec((at_once * size, given[1].shape[1]), lambda i, *_: (i, 0)),
            pl.BlockSpec((at_once, size, 2 * size), lambda i, *_: (i, 0, 0)),
        ]
    else:
        in_specs += state_specs
    for _ in pieces:
        if halves and half == 0:
            in_specs += [whole, whole]
        elif halves:
            in_specs.append(
                pl.BlockSpec((at_once * per, width), lambda i, *_: (jnp.minimum(i, half - 1), 0))
            )
            in_specs.append(pl.BlockSpec((at_once * per, width), lambda i, *_: (jnp.maximum(i - half, 0), 0)))
        else:
            in_specs.append(pl.BlockSpec((at_once * per, width), lambda i, *_: (i, 0)))
    operands = [lengths, shares, q, *given, *flat]
    scratch = [pltpu.VMEM((at_once, count, wide), BF16)]
    if finish:
        value = up_values.shape[2]
        operands.append(up_values)
        in_specs.append(whole)
        out_specs = pl.BlockSpec((total_rows, heads * value), lambda i, *_: (0, 0))
        out_shape = jax.ShapeDtypeStruct((total_rows, heads * value), BF16)
        scratch.append(pltpu.VMEM((heads, total_rows, latent), BF16))
    else:
        out_specs = state_specs
        out_shape = [
            jax.ShapeDtypeStruct((requests, rows, 128), F32),
            jax.ShapeDtypeStruct((requests, rows, 128), F32),
            jax.ShapeDtypeStruct((requests, rows, latent), BF16),
        ]
    return pl.pallas_call(
        functools.partial(attend_kernel, scale, picks, shared, halves, finish),
        grid_spec=pltpu.PrefetchScalarGridSpec(
            num_scalar_prefetch=2,
            grid=(requests // at_once,),
            in_specs=in_specs,
            out_specs=out_specs,
            scratch_shapes=scratch,
        ),
        out_shape=out_shape,
        input_output_aliases={} if shared or finish else {3: 0, 4: 1, 5: 2},
        cost_estimate=pl.CostEstimate(
            flops=2 * requests * rows * count * (2 * latent + 64),
            bytes_accessed=requests * rows * latent * 8,
            transcendentals=requests * rows * count,
        ),
        compiler_params=pltpu.CompilerParams(vmem_limit_bytes=VMEM_LIMIT),
        name=name,
    )(*operands)


def local(
    q_nope,
    q_rope,
    up_keys,
    up_values,
    page_pool,
    page_table,
    lengths,
    prefix_latent,
    tree_latent,
    parents,
):
    heads, nope_dim, latent_dim = up_keys.shape
    rope_dim = q_rope.shape[1] // heads
    scale = (nope_dim + rope_dim) ** (-0.5)
    groups = lax.axis_size("decode")
    shares = lax.axis_size("pool")
    pool_local = page_pool.shape[0]
    width = page_pool.shape[2]
    me = lax.axis_index("pool")

    flat = page_table.reshape(-1)
    entries = flat.shape[0]
    owner_of = flat // pool_local
    order = jnp.arange(entries, dtype=jnp.int32)
    owners = jnp.arange(groups, dtype=jnp.int32) * shares + me
    match = owner_of[None, :] == owners[:, None]
    code = order * pool_local + flat % pool_local
    first = jnp.min(jnp.where(match, code[None, :], entries * pool_local), axis=1)
    last = jnp.max(jnp.where(match, code[None, :], 0), axis=1)
    asks = jnp.stack([first, last], axis=1) % pool_local
    core = me % 2
    prompt = prefix_latent.reshape(-1, 128)
    held = prompt.shape[0] // 2
    prompt = jnp.where(core == 0, prompt[:held], prompt[held:])
    message, held_pool = compose(prompt, asks.astype(BF16), page_pool)
    message = lax.all_to_all(message, "decode", split_axis=0, concat_axis=0, tiled=True)
    wanted = message[:, held, :2].astype(jnp.int32)
    prefix = message[:, :held].reshape(-1, width)
    earlier = (order[None, :] < order[:, None]) & (owner_of[None, :] == owner_of[:, None])
    slot_of = jnp.any(earlier, axis=1).astype(jnp.int32)

    wide = latent_dim + 2 * rope_dim

    packed = pack(wanted, held_pool, shares)
    got = lax.all_to_all(packed, ("decode", "pool"), split_axis=0, concat_axis=0, tiled=True)
    q, hidden = prepare(q_nope, q_rope, up_keys, parents)
    tree = lax.optimization_barrier(jnp.pad(tree_latent, ((0, 0), (0, wide - width))))
    after = hidden[0, :1, :1] + (prefix[:1, :1] + tree[:1, :1]).astype(F32)
    own = compact(owner_of, slot_of, got, after).reshape(-1, 2 * width)

    swap = [(i, i ^ 1) for i in range(shares)]
    up = [(i, (i + 2) % shares) for i in range(shares)]
    down = [(i, (i - 2) % shares) for i in range(shares)]
    me = lax.axis_index("pool")
    other = me + 1 - 2 * (me % 2)
    at = [me, other, me - 2, me + 2, other - 2, other + 2, me + 4, other + 4]
    at = jnp.stack([place % shares for place in at]).astype(jnp.int32)
    def turn(array, pairs):
        return lax.ppermute(array, "pool", pairs)

    def call(name, picks, given, pieces, **more):
        return attend(
            name, scale, lengths, at, picks, q, name == "first", given, pieces, **more
        )

    below = turn(own, up)
    above = turn(own, down)
    beside = turn(own, swap)
    beside, prefix = lax.optimization_barrier((beside, prefix))
    prefix = jnp.concatenate([prefix, turn(prefix, swap)], axis=0)
    prefix = jnp.pad(prefix, ((0, 0), (0, wide - width)))
    state = call("first", (0, 1), (prefix, tree, hidden), [own, beside], at_once=2)
    below, above, state = lax.optimization_barrier((below, above, state))
    middle = own.shape[0] // 2
    far_low = turn(below[:middle], up)
    far_high = turn(above[middle:], down)
    state = call(
        "second",
        (2, 3, 4, 5),
        state,
        [below, above, turn(below, swap), turn(above, swap)],
        at_once=2,
    )
    far_low, far_high, state = lax.optimization_barrier((far_low, far_high, state))
    return call(
        "third",
        (6, 7),
        state,
        [(far_low, far_high), (turn(far_low, swap), turn(far_high, swap))],
        up_values=up_values,
        at_once=8,
    )


def solution(mesh):
    in_specs = (
        P("decode", "pool"),
        P("decode", "pool"),
        P("pool", None, None),
        P("pool", None, None),
        P(("decode", "pool"), None, None),
        P("decode", None),
        P("decode"),
        P("decode", None),
        P("decode", None),
        P("decode", None),
    )
    out_specs = P("decode", "pool")
    return jax.shard_map(local, mesh=mesh, in_specs=in_specs, out_specs=out_specs, check_vma=False)
```

```python
import functools
import math

import jax
import jax.numpy as jnp
from jax import lax
from jax.experimental import pallas as pl
from jax.experimental.pallas import tpu as pltpu
from jax.sharding import PartitionSpec as P

F32 = jnp.float32
BF16 = jnp.bfloat16
VMEM_LIMIT = 24 * 1024 * 1024


def nt_dot(a, b):
    return lax.dot_general(a, b, (((1,), (1,)), ((), ())), preferred_element_type=F32)


def prepare_kernel(rows_ref, rope_ref, keys_ref, parents_ref, q_ref, seen_ref):
    head = pl.program_id(0)
    latent = keys_ref.shape[2]
    absorbed = jnp.dot(rows_ref[...], keys_ref[0], preferred_element_type=F32)
    q_ref[0, :, :latent] = absorbed.astype(BF16)
    pair = rope_ref[...].astype(F32)
    lane = lax.broadcasted_iota(jnp.int32, pair.shape, 1)
    half = pair.shape[1] // 2
    turned = pltpu.roll(pair, half, 1)
    even = lax.rem(head, 2) == 0
    source = jnp.where(even, pair, turned)
    other = jnp.where(even, turned, pair)
    q_ref[0, :, latent : latent + 2 * half] = jnp.where(lane < half, source, 0.0).astype(BF16)
    q_ref[0, :, latent + 2 * half :] = jnp.where(lane >= half, other, 0.0).astype(BF16)
    size = parents_ref.shape[1]
    columns = lax.broadcasted_iota(jnp.int32, (size, size), 1)
    rows = lax.broadcasted_iota(jnp.int32, (size, size), 0)
    links = (parents_ref[0] == columns) | (rows == columns)
    reach = links.astype(F32)
    for sweep in range(max(1, (size - 1).bit_length())):
        reach = jnp.minimum(
            jnp.dot(reach.astype(BF16), reach.astype(BF16), preferred_element_type=F32), 1.0
        )
    lowest = jnp.full((size, size), -jnp.inf, F32)
    seen_ref[0] = jnp.concatenate([jnp.where(reach > 0.5, 0.0, lowest), lowest], axis=1)


def prepare(q_nope, q_rope, up_keys, parents):
    heads, nope, latent = up_keys.shape
    rows = q_nope.shape[0]
    requests, size = parents.shape
    rope = q_rope.shape[1] // heads
    return pl.pallas_call(
        prepare_kernel,
        grid=(heads,),
        in_specs=[
            pl.BlockSpec((rows, nope), lambda h: (0, h)),
            pl.BlockSpec((rows, 2 * rope), lambda h: (0, h // 2)),
            pl.BlockSpec((1, nope, latent), lambda h: (h, 0, 0)),
            pl.BlockSpec((1, size, 1), lambda h: (h, 0, 0)),
        ],
        out_specs=[
            pl.BlockSpec((1, rows, latent + 4 * rope), lambda h: (h, 0, 0)),
            pl.BlockSpec((1, size, 2 * size), lambda h: (h, 0, 0)),
        ],
        out_shape=[
            jax.ShapeDtypeStruct((heads, rows, latent + 4 * rope), BF16),
            jax.ShapeDtypeStruct((requests, size, 2 * size), F32),
        ],
        cost_estimate=pl.CostEstimate(
            flops=2 * rows * heads * nope * latent, bytes_accessed=10_000_000, transcendentals=0
        ),
        compiler_params=pltpu.CompilerParams(vmem_limit_bytes=VMEM_LIMIT),
        name="prepare",
    )(q_nope, q_rope, up_keys, parents[:, :, None])


def compose_kernel(held, prompt_ref, asks_ref, pool_ref, out_ref, pool_out_ref):
    prompt = prompt_ref[...].astype(F32)
    asks = asks_ref[...].astype(F32)
    rows = lax.broadcasted_iota(jnp.int32, prompt.shape, 0)
    for group in range(out_ref.shape[0]):
        out_ref[group] = jnp.where(rows == held, asks[group : group + 1, :], prompt).astype(BF16)


def compose(prompt, asks, pool):
    held = prompt.shape[0]
    rows = held + 16 - held % 16
    prompt = jnp.pad(prompt, ((0, rows - held), (0, 0)))
    asks = jnp.pad(asks, ((0, 0), (0, 126)))
    return pl.pallas_call(
        functools.partial(compose_kernel, held),
        in_specs=[pl.BlockSpec(memory_space=pltpu.VMEM)] * 3,
        out_specs=[pl.BlockSpec(memory_space=pltpu.VMEM)] * 2,
        out_shape=[
            jax.ShapeDtypeStruct((asks.shape[0], rows, 128), BF16),
            jax.ShapeDtypeStruct(pool.shape, pool.dtype),
        ],
        input_output_aliases={2: 1},
        cost_estimate=pl.CostEstimate(flops=0, bytes_accessed=1_000_000, transcendentals=0),
        compiler_params=pltpu.CompilerParams(vmem_limit_bytes=VMEM_LIMIT),
        name="compose",
    )(prompt, asks, pool)


def pack_kernel(wanted_ref, pool_ref, out_ref):
    size = pool_ref.shape[1]
    some = out_ref.shape[0] // size
    latent = 512
    for index in range(some):
        group = pl.program_id(0) * some + index
        first = pool_ref.at[wanted_ref[group, 0]]
        second = pool_ref.at[wanted_ref[group, 1]]
        rows = slice(index * size, (index + 1) * size)
        out_ref[rows, :latent] = first[:, :latent]
        out_ref[rows, latent : 2 * latent] = second[:, :latent]
        out_ref[rows, 2 * latent :] = jnp.concatenate(
            [first[:, latent:], second[:, latent:]], axis=1
        )


def pack(wanted, pool, shares):
    groups = wanted.shape[0]
    size, width = pool.shape[1:]
    steps = 2
    packed = pl.pallas_call(
        pack_kernel,
        grid=(steps,),
        in_specs=[
            pl.BlockSpec(memory_space=pltpu.SMEM),
            pl.BlockSpec(memory_space=pltpu.VMEM),
        ],
        out_specs=pl.BlockSpec((groups // steps * size, 2 * width), lambda i: (i, 0)),
        out_shape=pltpu.HBM((groups * size, 2 * width), BF16),
        cost_estimate=pl.CostEstimate(flops=0, bytes_accessed=5_000_000, transcendentals=0),
        compiler_params=pltpu.CompilerParams(vmem_limit_bytes=VMEM_LIMIT),
        name="pack",
    )(wanted, pool)
    return packed.reshape(groups * shares, size // shares, 2 * width)


def compact_kernel(source_ref, slot_ref, got_ref, after_ref, out_ref):
    pairs = out_ref.shape[0]
    per = 8
    latent = 512
    half = (out_ref.shape[2] - 2 * latent) // 2

    def body(k, carry):
        request = k // per
        first = request * (2 * per) + lax.rem(k, per)
        ropes = []
        for side, entry in enumerate((first, first + per)):
            source = source_ref[entry]
            slot = slot_ref[entry]
            start = pl.multiple_of(slot * latent, latent)
            out_ref[k, :, side * latent : (side + 1) * latent] = got_ref[
                source, :, pl.ds(start, latent)
            ]
            both = got_ref[source, :, 2 * latent :].astype(F32)
            ropes.append(jnp.where(slot == side, both, pltpu.roll(both, half, 1)))
        lane = lax.broadcasted_iota(jnp.int32, ropes[0].shape, 1)
        out_ref[k, :, 2 * latent :] = jnp.where(lane < half, ropes[0], ropes[1]).astype(BF16)
        return carry

    lax.fori_loop(0, pairs, body, 0, unroll=16)


def compact(source, slot, got, after):
    entries = source.shape[0]
    return pl.pallas_call(
        compact_kernel,
        in_specs=[
            pl.BlockSpec(memory_space=pltpu.SMEM),
            pl.BlockSpec(memory_space=pltpu.SMEM),
            pl.BlockSpec(memory_space=pltpu.VMEM),
            pl.BlockSpec(memory_space=pltpu.SMEM),
        ],
        out_specs=pl.BlockSpec(memory_space=pltpu.VMEM),
        out_shape=jax.ShapeDtypeStruct((entries // 2,) + got.shape[1:], BF16),
        cost_estimate=pl.CostEstimate(flops=0, bytes_accessed=4_000_000, transcendentals=0),
        compiler_params=pltpu.CompilerParams(vmem_limit_bytes=VMEM_LIMIT),
        name="compact",
    )(source, slot, got, after)


def spread(column, width):
    if width <= 128:
        return column[:, :width]
    return jnp.concatenate([column] * (width // 128), axis=1)


def attend_kernel(scale, picks, shared, halves, finish, lengths_ref, shares_ref, q_ref, *refs):
    refs = list(refs)
    taken = [refs.pop(0) for _ in range(3)]
    pieces = [
        (refs.pop(0), refs.pop(0)) if halves else (refs.pop(0),) for _ in range(len(picks))
    ]
    values_ref = refs.pop(0) if finish else None
    if finish:
        out_ref, keys_ref, mixed_ref, staged_ref, sems = refs
    else:
        top_out, total_out, sum_out, keys_ref = refs
    heads, total_rows, wide = q_ref.shape
    size = total_rows // lengths_ref.shape[0]
    latent = wide - 256
    whole = halves and keys_ref.shape[0] == lengths_ref.shape[0]
    part = pieces[0][0].shape[0] // 2 // keys_ref.shape[0] * (2 if whole else 1)
    section = len(picks) * part
    origin = keys_ref.shape[1] - 4 * section
    step_requests = keys_ref.shape[0]
    factor = scale * math.log2(math.e)
    lowest = F32(-jnp.inf)
    some = 8
    block = some * size

    @pl.when(pl.program_id(0) == 0)
    def _():
        for turn in range(step_requests):
            keys_ref[turn, :, latent:] = jnp.zeros((keys_ref.shape[1], 256), BF16)
            if shared:
                prompt = taken[0].shape[0]
                keys_ref[turn, :prompt, : latent + 128] = taken[0][...]
                keys_ref[turn, prompt + size : origin, :latent] = jnp.zeros(
                    (origin - prompt - size, latent), BF16
                )

    for turn in range(step_requests):
        if shared:
            prompt = taken[0].shape[0]
            keys_ref[turn, prompt : prompt + size, : latent + 128] = taken[1][turn * size : (turn + 1) * size]
        for which, refs_of in enumerate(pieces):
            half_of, place = divmod(turn, step_requests // 2) if whole else (0, turn)
            piece = refs_of[half_of][place * 2 * part : (place + 1) * 2 * part]
            if halves and not whole:
                piece = jnp.where(pl.program_id(0) < pl.num_programs(0) // 2, piece, refs_of[1][turn * 2 * part : (turn + 1) * 2 * part])
            for index in range(4):
                side, half = index // 2, index % 2
                rows = slice(
                    origin + index * section + which * part,
                    origin + index * section + (which + 1) * part,
                )
                some_rows = piece[half * part : (half + 1) * part]
                keys_ref[turn, rows, :latent] = some_rows[:, side * latent : (side + 1) * latent]
                keys_ref[turn, rows, latent + side * 128 : latent + (side + 1) * 128] = some_rows[
                    :, 2 * latent :
                ]

    def work(turn, request, length, sections):
        count = sections * section
        column = lax.broadcasted_iota(jnp.int32, (1, count), 1)
        position = column // section * 256 + column % part // 8 * 64 + column % 8
        for which, pick in enumerate(picks):
            position = position + jnp.where(
                column // part % len(picks) == which, shares_ref[pick] * 8, 0
            )
        bias = jnp.where(position < length, 0.0, lowest)
        if shared:
            hidden = jnp.concatenate([taken[2][turn]] * some, axis=0)
        for step in range(heads // some):
            which = slice(step * some, (step + 1) * some)
            rows = slice(step * block, (step + 1) * block)
            q = q_ref[which, pl.ds(pl.multiple_of(request * size, size), size), :]
            q = q.reshape(block, wide)
            scores = nt_dot(q, keys_ref[turn, origin : origin + count, :]) + bias
            if shared:
                first = nt_dot(q, keys_ref[turn, :prompt, :])
                tree = nt_dot(q, keys_ref[turn, prompt:origin, :]) + hidden
                scores = jnp.concatenate([first, tree, scores], axis=1)
            top = jnp.broadcast_to(jnp.max(scores, axis=1, keepdims=True), (block, 128))
            if not shared:
                before = taken[0][request, rows, :]
                top = jnp.maximum(top, before)
                fade = jnp.exp2((before - top) * factor)
            weights = jnp.exp2((scores - spread(top, scores.shape[1])) * factor)
            if finish:
                weights = weights.astype(BF16)
                ones = jnp.ones((weights.shape[1], 128), BF16)
                total = jnp.dot(weights, ones, preferred_element_type=F32)
            else:
                total = jnp.broadcast_to(jnp.sum(weights, axis=1, keepdims=True), (block, 128))
            mixed = jnp.dot(
                weights.astype(BF16),
                keys_ref[turn, 0 if shared else origin : origin + count, :latent],
                preferred_element_type=F32,
            )
            if not shared:
                total = total + taken[1][request, rows, :] * fade
                mixed = mixed + taken[2][request, rows, :].astype(F32) * spread(fade, latent)
            if finish:
                mixed = mixed * spread(1.0 / total, latent)
                mixed_ref[which, pl.ds(pl.multiple_of(request * size, size), size), :] = (
                    mixed.astype(BF16).reshape(some, size, latent)
                )
            else:
                top_out[request, rows, :] = top
                total_out[request, rows, :] = total
                sum_out[request, rows, :] = mixed.astype(BF16)

    steps = (4,) if step_requests > 1 else (1, 2, 3, 4) if section % 128 == 0 else (2, 4)
    for turn in range(step_requests):
        request = pl.program_id(0) * step_requests + turn
        length = lengths_ref[request]
        needed = pl.cdiv(length, 256)
        if len(steps) == 1:
            work(turn, request, length, steps[0])
        else:
            for low, high in zip((0,) + steps, steps):

                @pl.when((needed > low) & (needed <= high))
                def _():
                    work(turn, request, length, high)

    if finish:
        value = values_ref.shape[2]

        def leave(head):
            return pltpu.make_async_copy(
                staged_ref.at[head], out_ref.at[:, pl.ds(head * value, value)], sems.at[head]
            )

        @pl.when(pl.program_id(0) == pl.num_programs(0) - 1)
        def _():
            for head in range(heads):
                staged_ref[head] = jnp.dot(
                    mixed_ref[head], values_ref[head], preferred_element_type=F32
                ).astype(BF16)
                leave(head).start()
            for head in range(heads):
                leave(head).wait()


def attend(name, scale, lengths, shares, picks, q, shared, given, pieces, up_values=None, at_once=1):
    heads, total_rows, wide = q.shape
    requests = lengths.shape[0]
    size = total_rows // requests
    rows = heads * size
    latent = wide - 256
    halves = isinstance(pieces[0], tuple)
    finish = up_values is not None
    flat = [array for piece in pieces for array in (piece if halves else (piece,))]
    per = flat[0].shape[0] * (2 if halves else 1) // requests
    width = flat[0].shape[1]
    half = requests // 2 // at_once
    origin = given[0].shape[0] + 2 * size if shared else 0
    count = origin + 2 * per * len(pieces)

    whole = pl.BlockSpec(memory_space=pltpu.VMEM)
    state_specs = [whole, whole, whole]
    in_specs = [whole]
    if shared:
        in_specs += [
            pl.BlockSpec(given[0].shape, lambda i, *_: (0, 0)),
            pl.BlockSpec((at_once * size, given[1].shape[1]), lambda i, *_: (i, 0)),
            pl.BlockSpec((at_once, size, 2 * size), lambda i, *_: (i, 0, 0)),
        ]
    else:
        in_specs += state_specs
    for _ in pieces:
        if halves and half == 0:
            in_specs += [whole, whole]
        elif halves:
            in_specs.append(
                pl.BlockSpec((at_once * per, width), lambda i, *_: (jnp.minimum(i, half - 1), 0))
            )
            in_specs.append(pl.BlockSpec((at_once * per, width), lambda i, *_: (jnp.maximum(i - half, 0), 0)))
        else:
            in_specs.append(pl.BlockSpec((at_once * per, width), lambda i, *_: (i, 0)))
    operands = [lengths, shares, q, *given, *flat]
    scratch = [pltpu.VMEM((at_once, count, wide), BF16)]
    if finish:
        value = up_values.shape[2]
        operands.append(up_values)
        in_specs.append(whole)
        out_specs = pl.BlockSpec(memory_space=pltpu.HBM)
        out_shape = jax.ShapeDtypeStruct((total_rows, heads * value), BF16)
        staged = pltpu.VMEM((heads, total_rows, value), BF16)
        scratch += [pltpu.VMEM((heads, total_rows, latent), BF16), staged]
        scratch.append(pltpu.SemaphoreType.DMA((heads,)))
    else:
        out_specs = state_specs
        out_shape = [
            jax.ShapeDtypeStruct((requests, rows, 128), F32),
            jax.ShapeDtypeStruct((requests, rows, 128), F32),
            jax.ShapeDtypeStruct((requests, rows, latent), BF16),
        ]
    return pl.pallas_call(
        functools.partial(attend_kernel, scale, picks, shared, halves, finish),
        grid_spec=pltpu.PrefetchScalarGridSpec(
            num_scalar_prefetch=2,
            grid=(requests // at_once,),
            in_specs=in_specs,
            out_specs=out_specs,
            scratch_shapes=scratch,
        ),
        out_shape=out_shape,
        input_output_aliases={} if shared or finish else {3: 0, 4: 1, 5: 2},
        cost_estimate=pl.CostEstimate(
            flops=2 * requests * rows * count * (2 * latent + 64),
            bytes_accessed=requests * rows * latent * 8,
            transcendentals=requests * rows * count,
        ),
        compiler_params=pltpu.CompilerParams(vmem_limit_bytes=VMEM_LIMIT),
        name=name,
    )(*operands)


def local(
    q_nope,
    q_rope,
    up_keys,
    up_values,
    page_pool,
    page_table,
    lengths,
    prefix_latent,
    tree_latent,
    parents,
):
    heads, nope_dim, latent_dim = up_keys.shape
    rope_dim = q_rope.shape[1] // heads
    scale = (nope_dim + rope_dim) ** (-0.5)
    groups = lax.axis_size("decode")
    shares = lax.axis_size("pool")
    pool_local = page_pool.shape[0]
    width = page_pool.shape[2]
    me = lax.axis_index("pool")

    flat = page_table.reshape(-1)
    entries = flat.shape[0]
    owner_of = flat // pool_local
    order = jnp.arange(entries, dtype=jnp.int32)
    owners = jnp.arange(groups, dtype=jnp.int32) * shares + me
    match = owner_of[None, :] == owners[:, None]
    code = order * pool_local + flat % pool_local
    first = jnp.min(jnp.where(match, code[None, :], entries * pool_local), axis=1)
    last = jnp.max(jnp.where(match, code[None, :], 0), axis=1)
    asks = jnp.stack([first, last], axis=1) % pool_local
    core = me % 2
    prompt = prefix_latent.reshape(-1, 128)
    held = prompt.shape[0] // 2
    prompt = jnp.where(core == 0, prompt[:held], prompt[held:])
    message, held_pool = compose(prompt, asks.astype(BF16), page_pool)
    message = lax.all_to_all(message, "decode", split_axis=0, concat_axis=0, tiled=True)
    wanted = message[:, held, :2].astype(jnp.int32)
    prefix = message[:, :held].reshape(-1, width)
    earlier = (order[None, :] < order[:, None]) & (owner_of[None, :] == owner_of[:, None])
    slot_of = jnp.any(earlier, axis=1).astype(jnp.int32)

    wide = latent_dim + 2 * rope_dim

    packed = pack(wanted, held_pool, shares)
    got = lax.all_to_all(packed, ("decode", "pool"), split_axis=0, concat_axis=0, tiled=True)
    q, hidden = prepare(q_nope, q_rope, up_keys, parents)
    tree = lax.optimization_barrier(jnp.pad(tree_latent, ((0, 0), (0, wide - width))))
    after = hidden[0, :1, :1] + (prefix[:1, :1] + tree[:1, :1]).astype(F32)
    own = compact(owner_of, slot_of, got, after).reshape(-1, 2 * width)

    swap = [(i, i ^ 1) for i in range(shares)]
    up = [(i, (i + 2) % shares) for i in range(shares)]
    down = [(i, (i - 2) % shares) for i in range(shares)]
    me = lax.axis_index("pool")
    other = me + 1 - 2 * (me % 2)
    at = [me, other, me - 2, me + 2, other - 2, other + 2, me + 4, other + 4]
    at = jnp.stack([place % shares for place in at]).astype(jnp.int32)
    def turn(array, pairs):
        return lax.ppermute(array, "pool", pairs)

    def call(name, picks, given, pieces, **more):
        return attend(
            name, scale, lengths, at, picks, q, name == "first", given, pieces, **more
        )

    below = turn(own, up)
    above = turn(own, down)
    beside = turn(own, swap)
    beside, prefix = lax.optimization_barrier((beside, prefix))
    prefix = jnp.concatenate([prefix, turn(prefix, swap)], axis=0)
    prefix = jnp.pad(prefix, ((0, 0), (0, wide - width)))
    state = call("first", (0, 1), (prefix, tree, hidden), [own, beside], at_once=2)
    below, above, state = lax.optimization_barrier((below, above, state))
    middle = own.shape[0] // 2
    far_low = turn(below[:middle], up)
    far_high = turn(above[middle:], down)
    state = call(
        "second",
        (2, 3, 4, 5),
        state,
        [below, above, turn(below, swap), turn(above, swap)],
        at_once=2,
    )
    far_low, far_high, state = lax.optimization_barrier((far_low, far_high, state))
    return call(
        "third",
        (6, 7),
        state,
        [(far_low, far_high), (turn(far_low, swap), turn(far_high, swap))],
        up_values=up_values,
        at_once=8,
    )


def solution(mesh):
    in_specs = (
        P("decode", "pool"),
        P("decode", "pool"),
        P("pool", None, None),
        P("pool", None, None),
        P(("decode", "pool"), None, None),
        P("decode", None),
        P("decode"),
        P("decode", None),
        P("decode", None),
        P("decode", None),
    )
    out_specs = P("decode", "pool")
    return jax.shard_map(local, mesh=mesh, in_specs=in_specs, out_specs=out_specs, check_vma=False)
```
